32 devices in a mesh: lat: 4 (over z), lon: 4 (over y, x), mem: 2 (over core).
Axes of the slice: x: 2, y: 2, z: 4, core: 2. Of those that a mesh axis runs over, the one named last changes fastest.
Arguments:
- measured_inputs: bfloat16 [512, 128, 256], P(('lat', 'lon', 'mem')), may hold values from -6 to 6
- target_sector: int32 [512], P(('lat', 'lon', 'mem')), may hold values from 0 to 3, as said below
- hidden_member_fields: bfloat16 [2, 32, 32, 768], P('mem', 'lat', 'lon'), may hold values from -6 to 6
- analysis_adjoint: bfloat16 [2, 32, 32, 768], P('mem', 'lat', 'lon'), may hold values from -0.29882812 to 0.29882812
- inner_perceptron_coeffs: bfloat16 [256, 256], replicated, may hold values from -0.375 to 0.375
- outer_perceptron_coeffs: bfloat16 [256, 768], replicated, may hold values from -0.375 to 0.375
- probe_projector: bfloat16 [768, 768], replicated, may hold values from -0.21875 to 0.21875
- logit_sharpness: float32 [12], replicated, may hold values from 0.5 to 2.5
- adjacent_channel_coeffs: float32 [8, 768], replicated, may hold values from -0.7 to 0.7
Outputs:
- analysis: bfloat16 [2, 32, 32, 768], P('mem', 'lat', 'lon')
- in_weight_grad: float32 [256, 256], replicated
- out_weight_grad: float32 [256, 768], replicated
The draws below stay inside these ranges and needn't reach their ends.
Inputs may be any that keep to these rules, and one draw needn't show every extreme that they name: `target_sector`: of the 16 blocks of one device at most 8 have one destination, and one destination has exactly 8; in every band and member one sector receives exactly 8 blocks from every device of the band, 32 in all, and no sector receives more.
All inputs are finite; a program needn't handle non-finite values.
Results may differ from the reference program's by a relative error of at most 0.012.
The reference program's roundings to bfloat16 on the way count: a program that leaves them out, or rounds other values in their place, can miss the bound.
Values may be sent and summed in bfloat16 or wider, within the bound.
A program may use at most 192 MiB of HBM per device.

```python
import math
import jax
import jax.numpy as jnp
from jax import lax

DO = 256
HID = 256
D = 768
HEADS = 12
CHANNELS_PER_ATT = 64
BT = 128
CLAT = 8
CLON = 8
NB_DEV = 16
CAP = 8
TILE_CAP = 32
OBS_BLOCKS = 512
MEMBERS = 2
LATS = 32
LONS = 32
N_LAT = 4
N_LON = 4
N_MEM = 2


def shuffle_row(row_key, sector_row):
    return jax.random.permutation(row_key, sector_row)


def draw_target_sector(key, part):
    device_count = N_LAT * N_LON * N_MEM
    slot_count = N_LON * CAP
    first_key, second_key, third_key = jax.random.split(key, 3)
    hot_sector = jax.random.randint(first_key, (N_LAT, 1, N_MEM), 0, N_LON)
    hot_sector = jnp.broadcast_to(hot_sector, (N_LAT, N_LON, N_MEM)).reshape(device_count)
    slot_sector = jnp.arange(slot_count, dtype=jnp.int32) // CAP
    noise = jax.random.randint(second_key, (device_count, slot_count), 0, 1 << 20)
    priority = noise * slot_count + jnp.arange(slot_count, dtype=jnp.int32)[None, :]
    priority = jnp.where(slot_sector[None, :] == hot_sector[:, None], priority + (1 << 29), priority)
    unused, picked = lax.top_k(priority, NB_DEV)
    sectors = (picked // CAP).astype(jnp.int32)
    row_keys = jax.random.split(third_key, device_count)
    shuffled = jax.vmap(shuffle_row)(row_keys, sectors)
    return shuffled.reshape(device_count * NB_DEV).astype(jnp.int32)


def draw_logit_sharpness(key, part):
    first_key = jax.random.fold_in(key, 0)
    base_scale = jnp.exp(jax.random.uniform(first_key, (HEADS,), jnp.float32, jnp.log(0.5), jnp.log(2.5)))
    return base_scale.astype(jnp.float32)


def block_scale(own_key, shape, shards, low, top_value):
    loudness, own = 1.0, jax.random.fold_in(own_key, 6)
    for axis_at, parts in shards:
        draws = jnp.exp(jax.random.uniform(jax.random.fold_in(own, axis_at), (parts,), jnp.float32, low / len(shards), top_value / len(shards)))
        loudness = loudness * jnp.repeat(draws, shape[axis_at] // parts).reshape([-1 if axis == axis_at else 1 for axis in range(len(shape))])
    return loudness


def centred(key, shape, scale, reach, cuts=(), held_as=jnp.bfloat16):
    level = block_scale(key, shape, cuts, -0.22, 0.18) if cuts else 1.0
    drawn = jax.random.normal(key, shape, jnp.float32) * scale * level
    return jnp.minimum(jnp.maximum(drawn, -reach), reach).astype(held_as)


def setup_inputs(seed: int = 0) -> dict:
    key_list = jax.random.split(jax.random.key(seed), 10)
    measured_inputs = centred(key_list[0], (OBS_BLOCKS, BT, DO), 1.0, 6.0, ((0, 32),))
    target_sector = draw_target_sector(jax.random.fold_in(key_list[9], 71), 0)
    hidden_member_fields = centred(key_list[2], (MEMBERS, LATS, LONS, D), 1.0, 6.0, ((0, 2), (1, 4), (2, 4)))
    analysis_adjoint = centred(key_list[3], (MEMBERS, LATS, LONS, D), 0.05, 0.29882812, ((0, 2), (1, 4), (2, 4)))
    inner_perceptron_coeffs = centred(key_list[4], (DO, HID), DO ** -0.5, 0.375)
    outer_perceptron_coeffs = centred(key_list[5], (HID, D), HID ** -0.5, 0.375)
    probe_projector = centred(key_list[6], (D, D), D ** -0.5, 0.21875)
    logit_sharpness = draw_logit_sharpness(jax.random.fold_in(key_list[9], 71), 0)
    adjacent_channel_coeffs = jnp.clip(jax.random.uniform(key_list[8], (8, D), jnp.float32, -0.7, 0.7), -0.7, 0.7)
    return dict(measured_inputs=measured_inputs, target_sector=target_sector, hidden_member_fields=hidden_member_fields, analysis_adjoint=analysis_adjoint, inner_perceptron_coeffs=inner_perceptron_coeffs, outer_perceptron_coeffs=outer_perceptron_coeffs, probe_projector=probe_projector, logit_sharpness=logit_sharpness, adjacent_channel_coeffs=adjacent_channel_coeffs)


NEIGHBOURS = ((-1, -1), (-1, 0), (-1, 1), (0, -1), (0, 1), (1, -1), (1, 0), (1, 1))

def rounded(values):
    return lax.optimization_barrier(values.astype(jnp.bfloat16))

def silu_slope(pre_act):
    sigmoid_val = jax.nn.sigmoid(pre_act)
    return sigmoid_val * (1.0 + pre_act * (1.0 - sigmoid_val))

def neighbour_mix(field, adjacent_channel_coeffs, direction):
    values = field.astype(jnp.float32)
    n_rows = values.shape[1]
    n_cols = values.shape[2]
    padded = jnp.pad(values, ((0, 0), (1, 1), (0, 0), (0, 0)))
    padded = jnp.concatenate([padded[:, :, -1:], padded, padded[:, :, :1]], axis=2)
    total = values
    for offset_idx, (row_step, col_step) in enumerate(NEIGHBOURS):
        row_start = 1 + direction * row_step
        col_start = 1 + direction * col_step
        total = total + adjacent_channel_coeffs[offset_idx] * padded[:, row_start:row_start + n_rows, col_start:col_start + n_cols]
    return total

def mutual_attention_apply(probe_projection, grid_point_entries, lookup_projection_entries, genuine_entry_indicator, logit_sharpness):
    n_cells = grid_point_entries.shape[0]
    n_tokens = lookup_projection_entries.shape[0]
    query_heads = probe_projection.reshape(n_cells, HEADS, CHANNELS_PER_ATT).astype(jnp.float32)
    key_heads = lookup_projection_entries.reshape(n_tokens, HEADS, CHANNELS_PER_ATT).astype(jnp.float32)
    latent_heads = grid_point_entries.reshape(n_cells, HEADS, CHANNELS_PER_ATT).astype(jnp.float32)
    normaliser_entries = logit_sharpness / math.sqrt(CHANNELS_PER_ATT)
    scores = jnp.einsum('qhd,khd->hqk', query_heads, key_heads) * normaliser_entries[:, None, None]
    scores = jnp.where(genuine_entry_indicator[None, None, :], scores, -jnp.inf)
    self_score = jnp.einsum('qhd,qhd->hq', query_heads, latent_heads) * normaliser_entries[:, None]
    row_max = jnp.maximum(lax.optimization_barrier(jnp.max(scores, axis=2)), self_score)
    exp_terms = jnp.exp(scores - row_max[:, :, None])
    self_exp = jnp.exp(self_score - row_max)
    denominator = lax.optimization_barrier(jnp.sum(exp_terms, axis=2)) + self_exp
    probs = exp_terms / denominator[:, :, None]
    self_prob = self_exp / denominator
    weights = rounded(probs)
    self_weight = rounded(self_prob)
    update = jnp.einsum('hqk,khd->qhd', weights.astype(jnp.float32), key_heads)
    update = update + jnp.transpose(self_weight.astype(jnp.float32))[:, :, None] * latent_heads
    revised_analysis = rounded(grid_point_entries.astype(jnp.float32) + update.reshape(n_cells, HEADS * CHANNELS_PER_ATT))
    return (revised_analysis, (probs, self_prob, weights))

def mutual_attention_adjoint(probe_projection, grid_point_entries, lookup_projection_entries, retained_intermediates, hidden_field_adjoint, logit_sharpness):
    probs, self_prob, weights = retained_intermediates
    n_cells = grid_point_entries.shape[0]
    n_tokens = lookup_projection_entries.shape[0]
    query_heads = probe_projection.reshape(n_cells, HEADS, CHANNELS_PER_ATT).astype(jnp.float32)
    key_heads = lookup_projection_entries.reshape(n_tokens, HEADS, CHANNELS_PER_ATT).astype(jnp.float32)
    latent_heads = grid_point_entries.reshape(n_cells, HEADS, CHANNELS_PER_ATT).astype(jnp.float32)
    grad_heads = hidden_field_adjoint.reshape(n_cells, HEADS, CHANNELS_PER_ATT).astype(jnp.float32)
    normaliser_entries = logit_sharpness / math.sqrt(CHANNELS_PER_ATT)
    weight_grad = jnp.einsum('qhd,khd->hqk', grad_heads, key_heads)
    self_grad = jnp.einsum('qhd,qhd->hq', grad_heads, latent_heads)
    row_total = lax.optimization_barrier(jnp.sum(probs * weight_grad, axis=2)) + self_prob * self_grad
    logit_grad = rounded(probs * (weight_grad - row_total[:, :, None]) * normaliser_entries[:, None, None])
    measured_embedding_adjoint = jnp.einsum('hqk,qhd->khd', weights.astype(jnp.float32), grad_heads)
    measured_embedding_adjoint = measured_embedding_adjoint + jnp.einsum('hqk,qhd->khd', logit_grad.astype(jnp.float32), query_heads)
    return rounded(measured_embedding_adjoint.reshape(n_tokens, HEADS * CHANNELS_PER_ATT))

def reference(measured_inputs, target_sector, hidden_member_fields, analysis_adjoint, inner_perceptron_coeffs, outer_perceptron_coeffs, probe_projector, logit_sharpness, adjacent_channel_coeffs):
    n_cells = CLAT * CLON
    state_grad_grid = rounded(neighbour_mix(analysis_adjoint, adjacent_channel_coeffs, -1))
    blocks = measured_inputs.reshape(N_LAT, N_LON, N_MEM, NB_DEV, BT, DO).transpose(2, 0, 1, 3, 4, 5)
    blocks = blocks.reshape(N_MEM * N_LAT, N_LON * NB_DEV, BT, DO)
    targets = target_sector.reshape(N_LAT, N_LON, N_MEM, NB_DEV).transpose(2, 0, 1, 3)
    targets = targets.reshape(N_MEM * N_LAT, N_LON * NB_DEV)

    def to_tiles(grid):
        tiles = grid.reshape(N_MEM, N_LAT, CLAT, N_LON, CLON, D).transpose(0, 1, 3, 2, 4, 5)
        return tiles.reshape(N_MEM * N_LAT, N_LON, n_cells, D)
    latent_tiles = to_tiles(hidden_member_fields)
    grad_tiles = to_tiles(state_grad_grid)
    slot_ids = jnp.arange(TILE_CAP * BT, dtype=jnp.int32) // BT
    sector_ids = jnp.arange(N_LON, dtype=jnp.int32)

    def one_band(band_args):
        band_blocks, band_targets, band_latent, band_grad = band_args
        order = jnp.argsort(band_targets, stable=True).astype(jnp.int32)
        sorted_blocks = jnp.concatenate([band_blocks[order], jnp.zeros((TILE_CAP, BT, DO), band_blocks.dtype)], axis=0)
        all_tokens = sorted_blocks.reshape(-1, DO)
        pre_act = jnp.dot(all_tokens, inner_perceptron_coeffs, preferred_element_type=jnp.float32)
        hidden_act = rounded(jax.nn.silu(pre_act))
        obs_feat = rounded(jnp.dot(hidden_act, outer_perceptron_coeffs, preferred_element_type=jnp.float32))
        counts = lax.optimization_barrier(jnp.sum((band_targets[None, :] == sector_ids[:, None]).astype(jnp.int32), axis=1))
        starts = (jnp.cumsum(counts) - counts).astype(jnp.int32)

        def one_tile(carry, tile_args):
            start, count, patchwise_hidden, patchwise_adjoint = tile_args
            token_start = (start * BT).astype(jnp.int32)
            lookup_projection_entries = lax.dynamic_slice_in_dim(obs_feat, token_start, TILE_CAP * BT, 0)
            genuine_entry_indicator = slot_ids < count
            probe_projection = rounded(jnp.dot(patchwise_hidden, probe_projector, preferred_element_type=jnp.float32))
            revised_analysis, retained_intermediates = mutual_attention_apply(probe_projection, patchwise_hidden, lookup_projection_entries, genuine_entry_indicator, logit_sharpness)
            measured_embedding_adjoint = mutual_attention_adjoint(probe_projection, patchwise_hidden, lookup_projection_entries, retained_intermediates, patchwise_adjoint, logit_sharpness)
            current = lax.dynamic_slice_in_dim(carry, token_start, TILE_CAP * BT, 0)
            carry = lax.dynamic_update_slice_in_dim(carry, current + measured_embedding_adjoint, token_start, 0)
            return (carry, revised_analysis)
        start_grad = jnp.zeros(((N_LON * NB_DEV + TILE_CAP) * BT, D), jnp.bfloat16)
        feature_all, states = lax.scan(one_tile, start_grad, (starts, counts, band_latent, band_grad))
        hidden_grad = rounded(jnp.dot(feature_all, outer_perceptron_coeffs.T, preferred_element_type=jnp.float32) * silu_slope(pre_act))
        out_grad = jnp.dot(hidden_act.T, feature_all, preferred_element_type=jnp.float32)
        in_grad = jnp.dot(all_tokens.T, hidden_grad, preferred_element_type=jnp.float32)
        return (states, in_grad, out_grad)
    states, in_parts, out_parts = lax.map(one_band, (blocks, targets, latent_tiles, grad_tiles))
    state_grid = states.reshape(N_MEM, N_LAT, N_LON, CLAT, CLON, D).transpose(0, 1, 3, 2, 4, 5)
    state_grid = state_grid.reshape(N_MEM, LATS, LONS, D)
    analysis = rounded(neighbour_mix(state_grid, adjacent_channel_coeffs, 1))
    return (analysis, lax.optimization_barrier(jnp.sum(in_parts, axis=0)), lax.optimization_barrier(jnp.sum(out_parts, axis=0)))
```

```python
import functools
import math

import jax
import jax.numpy as jnp
from jax import lax
from jax.experimental import pallas as pl
from jax.experimental.pallas import tpu as pltpu
from jax.sharding import PartitionSpec as P

HEADS = 12
CHANNELS_PER_ATT = 64


NEIGHBOURS = ((-1, -1), (-1, 0), (-1, 1), (0, -1), (0, 1), (1, -1), (1, 0), (1, 1))


def extended(block, sides, width):
    for axis, dim in sides:
        count = lax.axis_size(axis)
        forward = [(i, i + 1) for i in range(count - 1)]
        forward.append((count - 1, 0))
        backward = [(target, source) for source, target in forward]
        low = lax.ppermute(
            lax.slice_in_dim(block, block.shape[dim] - width, None, axis=dim), axis, forward
        )
        high = lax.ppermute(lax.slice_in_dim(block, 0, width, axis=dim), axis, backward)
        block = jnp.concatenate([low, block, high], axis=dim)
    return block


def silu_slope(pre_act):
    sigmoid_val = jax.nn.sigmoid(pre_act)
    return sigmoid_val * (1.0 + pre_act * (1.0 - sigmoid_val))


def mix_local(padded, keep_rows, adjacent_channel_coeffs, direction):
    values = padded.astype(jnp.float32) * keep_rows[:, None, None]
    n_rows = padded.shape[0] - 2
    n_cols = padded.shape[1] - 2
    total = values[1 : 1 + n_rows, 1 : 1 + n_cols]
    for offset_idx, (row_step, col_step) in enumerate(NEIGHBOURS):
        row_start = 1 + direction * row_step
        col_start = 1 + direction * col_step
        total = (
            total
            + adjacent_channel_coeffs[offset_idx]
            * values[row_start : row_start + n_rows, col_start : col_start + n_cols]
        )
    return total


def mutual_attention_apply(
    probe_projection,
    grid_point_entries,
    lookup_projection_entries,
    genuine_entry_indicator,
    logit_sharpness,
):
    n_cells = grid_point_entries.shape[0]
    n_tokens = lookup_projection_entries.shape[0]
    query_heads = probe_projection.reshape(n_cells, HEADS, CHANNELS_PER_ATT)
    key_heads = lookup_projection_entries.reshape(n_tokens, HEADS, CHANNELS_PER_ATT)
    latent_heads = grid_point_entries.reshape(n_cells, HEADS, CHANNELS_PER_ATT)
    normaliser_entries = logit_sharpness / math.sqrt(CHANNELS_PER_ATT)
    scores = jnp.einsum("qhd,khd->hqk", query_heads, key_heads, preferred_element_type=jnp.float32)
    scores = jnp.where(
        genuine_entry_indicator[None, None, :], scores * normaliser_entries[:, None, None], -jnp.inf
    )
    self_score = jnp.einsum(
        "qhd,qhd->hq", query_heads, latent_heads, preferred_element_type=jnp.float32
    )
    self_score = self_score * normaliser_entries[:, None]
    row_max = jnp.maximum(jnp.max(scores, axis=2), self_score)
    exp_terms = jnp.exp(scores - row_max[:, :, None])
    self_exp = jnp.exp(self_score - row_max)
    denominator = jnp.sum(exp_terms, axis=2) + self_exp
    probs = exp_terms / denominator[:, :, None]
    self_prob = self_exp / denominator
    weights = probs.astype(jnp.bfloat16)
    self_weight = lax.optimization_barrier(self_prob.astype(jnp.bfloat16)).astype(jnp.float32)
    update = jnp.einsum("hqk,khd->qhd", weights, key_heads, preferred_element_type=jnp.float32)
    update = update + jnp.transpose(self_weight)[:, :, None] * latent_heads.astype(jnp.float32)
    revised_analysis = (
        grid_point_entries.astype(jnp.float32) + update.reshape(n_cells, HEADS * CHANNELS_PER_ATT)
    ).astype(jnp.bfloat16)
    return (revised_analysis, (probs, self_prob, weights))


def mutual_attention_adjoint(
    probe_projection,
    grid_point_entries,
    lookup_projection_entries,
    retained_intermediates,
    hidden_field_adjoint,
    logit_sharpness,
):
    probs, self_prob, weights = retained_intermediates
    n_cells = grid_point_entries.shape[0]
    n_tokens = lookup_projection_entries.shape[0]
    query_heads = probe_projection.reshape(n_cells, HEADS, CHANNELS_PER_ATT)
    key_heads = lookup_projection_entries.reshape(n_tokens, HEADS, CHANNELS_PER_ATT)
    latent_heads = grid_point_entries.reshape(n_cells, HEADS, CHANNELS_PER_ATT)
    grad_heads = hidden_field_adjoint.reshape(n_cells, HEADS, CHANNELS_PER_ATT)
    normaliser_entries = logit_sharpness / math.sqrt(CHANNELS_PER_ATT)
    weight_grad = jnp.einsum(
        "qhd,khd->hqk", grad_heads, key_heads, preferred_element_type=jnp.float32
    )
    self_grad = jnp.einsum(
        "qhd,qhd->hq", grad_heads, latent_heads, preferred_element_type=jnp.float32
    )
    row_total = jnp.sum(probs * weight_grad, axis=2) + self_prob * self_grad
    logit_grad = (
        probs * (weight_grad - row_total[:, :, None]) * normaliser_entries[:, None, None]
    ).astype(jnp.bfloat16)
    measured_embedding_adjoint = jnp.einsum(
        "hqk,qhd->khd", weights, grad_heads, preferred_element_type=jnp.float32
    )
    measured_embedding_adjoint = measured_embedding_adjoint + jnp.einsum(
        "hqk,qhd->khd", logit_grad, query_heads, preferred_element_type=jnp.float32
    )
    return measured_embedding_adjoint.reshape(n_tokens, HEADS * CHANNELS_PER_ATT).astype(
        jnp.bfloat16
    )

MESH = pl.DeviceIdType.MESH


def sum_scratch(n_lat, n_lon, rows, width):
    half = rows // 2
    part = half // n_lon
    return [
        pltpu.VMEM((rows, width), jnp.bfloat16),
        pltpu.VMEM((half, width), jnp.bfloat16),
        pltpu.VMEM((half, width), jnp.float32),
        pltpu.VMEM((n_lon, part, width), jnp.bfloat16),
        pltpu.VMEM((n_lon, part, width), jnp.bfloat16),
        pltpu.VMEM((n_lat, part, width), jnp.bfloat16),
        pltpu.VMEM((2, half, width), jnp.bfloat16),
        pltpu.SemaphoreType.DMA((2,)),
        pltpu.SemaphoreType.DMA((2,)),
        pltpu.SemaphoreType.DMA((2, n_lon)),
        pltpu.SemaphoreType.DMA((2, n_lon)),
        pltpu.SemaphoreType.DMA((n_lat,)),
        pltpu.SemaphoreType.DMA((n_lat,)),
    ]


def sum_over_devices(total, n_lat, n_lon, scratch):
    (rounded, from_core, half_sum, to_lon, from_lon, by_lat, whole,
     core_send, core_recv, lon_send, lon_recv, lat_send, lat_recv) = scratch
    lat, lon, mem = (lax.axis_index(name) for name in ("lat", "lon", "mem"))
    other = 1 - mem
    rows = total.shape[0]
    half = rows // 2
    part = half // n_lon

    rounded[...] = total[...].astype(jnp.bfloat16)
    away = pl.ds(pl.multiple_of(other * half, half), half)
    copy = pltpu.make_async_remote_copy(
        src_ref=rounded.at[away], dst_ref=from_core,
        send_sem=core_send.at[0], recv_sem=core_recv.at[0],
        device_id=(lat, lon, other), device_id_type=MESH)
    copy.start()
    copy.wait()
    mine = pl.ds(pl.multiple_of(mem * half, half), half)
    half_sum[...] = total[mine, :] + from_core[...].astype(jnp.float32)

    to_lon[...] = half_sum[...].astype(jnp.bfloat16).reshape(to_lon.shape)
    copies = []
    for step in range(1, n_lon):
        peer = lax.rem(lon + step, n_lon)
        copy = pltpu.make_async_remote_copy(
            src_ref=to_lon.at[peer], dst_ref=from_lon.at[step],
            send_sem=lon_send.at[0, step], recv_sem=lon_recv.at[0, step],
            device_id=(lat, peer, mem), device_id_type=MESH)
        copy.start()
        copies.append(copy)
    part_sum = half_sum[pl.ds(pl.multiple_of(lon * part, part), part), :]
    for step, copy in enumerate(copies, 1):
        copy.wait()
        part_sum = part_sum + from_lon[step].astype(jnp.float32)

    by_lat[lat] = part_sum.astype(jnp.bfloat16)
    copies = []
    for step in range(1, n_lat):
        peer = lax.rem(lat + step, n_lat)
        copy = pltpu.make_async_remote_copy(
            src_ref=by_lat.at[lat], dst_ref=by_lat.at[lat],
            send_sem=lat_send.at[step], recv_sem=lat_recv.at[step],
            device_id=(peer, lon, mem), device_id_type=MESH)
        copy.start()
        copies.append(copy)
    for copy in copies:
        copy.wait()
    band_sum = by_lat[0].astype(jnp.float32)
    for index in range(1, n_lat):
        band_sum = band_sum + by_lat[index].astype(jnp.float32)

    own = pl.ds(pl.multiple_of(lon * part, part), part)
    whole[mem, own, :] = band_sum.astype(jnp.bfloat16)
    copies = []
    for step in range(1, n_lon):
        peer = lax.rem(lon + step, n_lon)
        copy = pltpu.make_async_remote_copy(
            src_ref=whole.at[mem, own], dst_ref=whole.at[mem, own],
            send_sem=lon_send.at[1, step], recv_sem=lon_recv.at[1, step],
            device_id=(lat, peer, mem), device_id_type=MESH)
        copy.start()
        copies.append(copy)
    for copy in copies:
        copy.wait()
    copy = pltpu.make_async_remote_copy(
        src_ref=whole.at[mem], dst_ref=whole.at[mem],
        send_sem=core_send.at[1], recv_sem=core_recv.at[1],
        device_id=(lat, lon, other), device_id_type=MESH)
    copy.start()
    copy.wait()
    return whole


def greet(partners):
    barrier = pltpu.get_barrier_semaphore()
    for partner in partners:
        pl.semaphore_signal(barrier, inc=1, device_id=partner, device_id_type=MESH)
    pl.semaphore_wait(barrier, len(partners))


def sum_partners(n_lat, n_lon):
    lat, lon, mem = (lax.axis_index(name) for name in ("lat", "lon", "mem"))
    partners = [(lat, lon, 1 - mem)]
    partners += [(lat, lax.rem(lon + step, n_lon), mem) for step in range(1, n_lon)]
    partners += [(lax.rem(lat + step, n_lat), lon, mem) for step in range(1, n_lat)]
    return partners


def sum_kernel(n_lat, n_lon, in_ref, out_ref, in_sum, out_sum, total, *scratch):
    greet(sum_partners(n_lat, n_lon))
    rows, wide = in_ref.shape
    total[:rows, :wide] = in_ref[...]
    total[:rows, wide:] = out_ref[:, :wide]
    total[rows:, :] = out_ref[:, wide:]
    whole = sum_over_devices(total, n_lat, n_lon, scratch)
    in_sum[...] = whole[0, :, :wide].astype(jnp.float32)
    out_sum[:, :wide] = whole[0, :, wide:].astype(jnp.float32)
    out_sum[:, wide:] = whole[1].astype(jnp.float32)


def summed(in_grad, out_grad):
    n_lat, n_lon = lax.axis_size("lat"), lax.axis_size("lon")
    rows, width = 2 * in_grad.shape[0], 2 * in_grad.shape[1]
    return pl.pallas_call(
        functools.partial(sum_kernel, n_lat, n_lon),
        out_shape=[
            jax.ShapeDtypeStruct(in_grad.shape, jnp.float32),
            jax.ShapeDtypeStruct(out_grad.shape, jnp.float32),
        ],
        in_specs=[pl.BlockSpec(memory_space=pltpu.VMEM)] * 2,
        out_specs=[pl.BlockSpec(memory_space=pltpu.VMEM)] * 2,
        scratch_shapes=[pltpu.VMEM((rows, width), jnp.float32)]
        + sum_scratch(n_lat, n_lon, rows, width),
        compiler_params=pltpu.CompilerParams(
            collective_id=0, has_side_effects=True, vmem_limit_bytes=32 << 20
        ),
        name="sum_over_devices",
    )(in_grad, out_grad)


def per_device(
    measured_inputs,
    target_sector,
    hidden_member_fields,
    analysis_adjoint,
    inner_perceptron_coeffs,
    outer_perceptron_coeffs,
    probe_projector,
    logit_sharpness,
    adjacent_channel_coeffs,
):
    lon_count = lax.axis_size("lon")
    lat_count = lax.axis_size("lat")
    block_count = target_sector.shape[0]
    block_len = measured_inputs.shape[1]
    obs_width = measured_inputs.shape[2]
    model_width = hidden_member_fields.shape[3]
    hidden_width = inner_perceptron_coeffs.shape[1]
    cell_rows = hidden_member_fields.shape[1]
    cell_cols = hidden_member_fields.shape[2]
    n_cells = cell_rows * cell_cols
    cap_slots = max(2, 2 * block_count // lon_count)
    sector_ids = jnp.arange(lon_count, dtype=jnp.int32)
    one_hot = (target_sector[:, None] == sector_ids[None, :]).astype(jnp.int32)
    earlier = jnp.cumsum(one_hot, axis=0) - one_hot
    slot_index = target_sector * cap_slots + jnp.sum(earlier * one_hot, axis=1)
    cot_padded = extended(analysis_adjoint[0], (("lat", 0), ("lon", 1)), 1)
    band_targets = lax.all_gather(target_sector, "lon", axis=0, tiled=True)
    own_sector = lax.axis_index("lon")
    arrivals = jnp.sum(
        (band_targets == own_sector).astype(jnp.int32).reshape(lon_count, block_count), axis=1
    )
    live_slots = jnp.arange(cap_slots, dtype=jnp.int32)[None, :] < arrivals[:, None]
    genuine_entry_indicator = jnp.broadcast_to(
        live_slots[:, :, None], (lon_count, cap_slots, block_len)
    ).reshape(-1)
    grid_point_entries = hidden_member_fields.reshape(n_cells, model_width)
    probe_projection = jnp.dot(
        grid_point_entries, probe_projector, preferred_element_type=jnp.float32
    ).astype(jnp.bfloat16)
    send_blocks = jnp.zeros((lon_count * cap_slots, block_len, obs_width), jnp.bfloat16)
    send_blocks = (
        send_blocks.at[slot_index]
        .set(measured_inputs)
        .reshape(lon_count, cap_slots, block_len, obs_width)
    )
    obs_blocks = lax.all_to_all(send_blocks, "lon", split_axis=0, concat_axis=0, tiled=True)
    pre_act = jnp.dot(obs_blocks, inner_perceptron_coeffs, preferred_element_type=jnp.float32)
    hidden_act = jax.nn.silu(pre_act).astype(jnp.bfloat16)
    obs_feat = jnp.dot(
        hidden_act, outer_perceptron_coeffs, preferred_element_type=jnp.float32
    ).astype(jnp.bfloat16)
    token_blocks, pre_act, hidden_act, obs_feat = (obs_blocks, pre_act, hidden_act, obs_feat)
    lookup_projection_entries = obs_feat.reshape(-1, model_width)
    revised_analysis, retained_intermediates = mutual_attention_apply(
        probe_projection,
        grid_point_entries,
        lookup_projection_entries,
        genuine_entry_indicator,
        logit_sharpness,
    )
    state_grid = revised_analysis.reshape(cell_rows, cell_cols, model_width)
    state_padded = extended(state_grid, (("lat", 0), ("lon", 1)), 1)
    lat_index = lax.axis_index("lat")
    keep_rows = jnp.ones((cell_rows + 2,), jnp.float32)
    keep_rows = keep_rows.at[0].set(jnp.where(lat_index > 0, 1.0, 0.0))
    keep_rows = keep_rows.at[cell_rows + 1].set(jnp.where(lat_index < lat_count - 1, 1.0, 0.0))
    analysis = (
        mix_local(state_padded, keep_rows, adjacent_channel_coeffs, 1)
        .astype(jnp.bfloat16)
        .reshape(hidden_member_fields.shape)
    )
    hidden_field_adjoint = (
        mix_local(cot_padded, keep_rows, adjacent_channel_coeffs, -1)
        .astype(jnp.bfloat16)
        .reshape(n_cells, model_width)
    )
    measured_embedding_adjoint = mutual_attention_adjoint(
        probe_projection,
        grid_point_entries,
        lookup_projection_entries,
        retained_intermediates,
        hidden_field_adjoint,
        logit_sharpness,
    )
    grad_blocks = measured_embedding_adjoint.reshape(lon_count, cap_slots, block_len, model_width)
    grad_rows = grad_blocks.reshape(-1, model_width)
    hidden_rows = hidden_act.reshape(-1, hidden_width)
    pre_rows = pre_act.reshape(-1, hidden_width)
    hidden_grad = jnp.einsum(
        "td,hd->th", grad_rows, outer_perceptron_coeffs, preferred_element_type=jnp.float32
    )
    hidden_grad = (hidden_grad * silu_slope(pre_rows)).astype(jnp.bfloat16)
    out_grad = jnp.einsum("th,td->hd", hidden_rows, grad_rows, preferred_element_type=jnp.float32)
    in_grad = jnp.einsum(
        "tc,th->ch",
        token_blocks.reshape(-1, obs_width),
        hidden_grad,
        preferred_element_type=jnp.float32,
    )
    in_grad, out_grad = summed(in_grad, out_grad)
    return (analysis, in_grad, out_grad)


def solution(mesh):
    in_specs = (
        P(("lat", "lon", "mem"), None, None),
        P(("lat", "lon", "mem")),
        P("mem", "lat", "lon", None),
        P("mem", "lat", "lon", None),
        P(),
        P(),
        P(),
        P(),
        P(),
    )
    out_specs = (P("mem", "lat", "lon", None), P(), P())
    return jax.shard_map(
        per_device, mesh=mesh, in_specs=in_specs, out_specs=out_specs, check_vma=False
    )
```

```python
import functools
import math

import jax
import jax.numpy as jnp
from jax import lax
from jax.experimental import pallas as pl
from jax.experimental.pallas import tpu as pltpu
from jax.sharding import PartitionSpec as P

HEADS = 12
CHANNELS_PER_ATT = 64
GROUP = 256
CHUNK = 512
LOWEST = -1e30


NEIGHBOURS = ((-1, -1), (-1, 0), (-1, 1), (0, -1), (0, 1), (1, -1), (1, 0), (1, 1))

MESH = pl.DeviceIdType.MESH


def sum_scratch(n_lat, n_lon, rows, width):
    half = rows // 2
    part = half // n_lon
    return [
        pltpu.VMEM((rows, width), jnp.bfloat16),
        pltpu.VMEM((half, width), jnp.bfloat16),
        pltpu.VMEM((half, width), jnp.float32),
        pltpu.VMEM((n_lon, part, width), jnp.bfloat16),
        pltpu.VMEM((n_lon, part, width), jnp.bfloat16),
        pltpu.VMEM((n_lat, part, width), jnp.bfloat16),
        pltpu.VMEM((2, half, width), jnp.bfloat16),
        pltpu.SemaphoreType.DMA((2,)),
        pltpu.SemaphoreType.DMA((2,)),
        pltpu.SemaphoreType.DMA((2, n_lon)),
        pltpu.SemaphoreType.DMA((2, n_lon)),
        pltpu.SemaphoreType.DMA((n_lat,)),
        pltpu.SemaphoreType.DMA((n_lat,)),
    ]


def sum_over_devices(total, n_lat, n_lon, scratch):
    (rounded, from_core, half_sum, to_lon, from_lon, by_lat, whole,
     core_send, core_recv, lon_send, lon_recv, lat_send, lat_recv) = scratch
    lat, lon, mem = (lax.axis_index(name) for name in ("lat", "lon", "mem"))
    other = 1 - mem
    rows = total.shape[0]
    half = rows // 2
    part = half // n_lon

    rounded[...] = total[...].astype(jnp.bfloat16)
    away = pl.ds(pl.multiple_of(other * half, half), half)
    copy = pltpu.make_async_remote_copy(
        src_ref=rounded.at[away], dst_ref=from_core,
        send_sem=core_send.at[0], recv_sem=core_recv.at[0],
        device_id=(lat, lon, other), device_id_type=MESH)
    copy.start()
    copy.wait()
    mine = pl.ds(pl.multiple_of(mem * half, half), half)
    half_sum[...] = total[mine, :] + from_core[...].astype(jnp.float32)

    to_lon[...] = half_sum[...].astype(jnp.bfloat16).reshape(to_lon.shape)
    copies = []
    for step in range(1, n_lon):
        peer = lax.rem(lon + step, n_lon)
        copy = pltpu.make_async_remote_copy(
            src_ref=to_lon.at[peer], dst_ref=from_lon.at[step],
            send_sem=lon_send.at[0, step], recv_sem=lon_recv.at[0, step],
            device_id=(lat, peer, mem), device_id_type=MESH)
        copy.start()
        copies.append(copy)
    part_sum = half_sum[pl.ds(pl.multiple_of(lon * part, part), part), :]
    for step, copy in enumerate(copies, 1):
        copy.wait()
        part_sum = part_sum + from_lon[step].astype(jnp.float32)

    by_lat[lat] = part_sum.astype(jnp.bfloat16)
    copies = []
    for step in range(1, n_lat):
        peer = lax.rem(lat + step, n_lat)
        copy = pltpu.make_async_remote_copy(
            src_ref=by_lat.at[lat], dst_ref=by_lat.at[lat],
            send_sem=lat_send.at[step], recv_sem=lat_recv.at[step],
            device_id=(peer, lon, mem), device_id_type=MESH)
        copy.start()
        copies.append(copy)
    for copy in copies:
        copy.wait()
    band_sum = by_lat[0].astype(jnp.float32)
    for index in range(1, n_lat):
        band_sum = band_sum + by_lat[index].astype(jnp.float32)

    own = pl.ds(pl.multiple_of(lon * part, part), part)
    whole[mem, own, :] = band_sum.astype(jnp.bfloat16)
    copies = []
    for step in range(1, n_lon):
        peer = lax.rem(lon + step, n_lon)
        copy = pltpu.make_async_remote_copy(
            src_ref=whole.at[mem, own], dst_ref=whole.at[mem, own],
            send_sem=lon_send.at[1, step], recv_sem=lon_recv.at[1, step],
            device_id=(lat, peer, mem), device_id_type=MESH)
        copy.start()
        copies.append(copy)
    for copy in copies:
        copy.wait()
    copy = pltpu.make_async_remote_copy(
        src_ref=whole.at[mem], dst_ref=whole.at[mem],
        send_sem=core_send.at[1], recv_sem=core_recv.at[1],
        device_id=(lat, lon, other), device_id_type=MESH)
    copy.start()
    copy.wait()
    return whole


def greet(partners):
    barrier = pltpu.get_barrier_semaphore()
    for partner in partners:
        pl.semaphore_signal(barrier, inc=1, device_id=partner, device_id_type=MESH)
    pl.semaphore_wait(barrier, len(partners))


def rows_of(index, size):
    return pl.ds(pl.multiple_of(index * size, size), size)


def lanes_of(group):
    return slice(group * GROUP, (group + 1) * GROUP)


def dot(left, right):
    return jnp.dot(left, right, preferred_element_type=jnp.float32)


def dot_rows(left, right):
    return lax.dot_general(
        left, right, (((0,), (0,)), ((), ())), preferred_element_type=jnp.float32
    )


def spread_heads(cells):
    tall = jnp.concatenate([cells] * (GROUP // CHANNELS_PER_ATT), axis=0)
    row_head = lax.broadcasted_iota(jnp.int32, tall.shape, 0) // cells.shape[0]
    col_head = lax.broadcasted_iota(jnp.int32, tall.shape, 1) // CHANNELS_PER_ATT
    return jnp.where(row_head == col_head, tall, 0.0)


def gather_heads(tall, n_cells):
    col_head = lax.broadcasted_iota(jnp.int32, (n_cells, GROUP), 1) // CHANNELS_PER_ATT
    cells = tall[:n_cells]
    for head in range(1, GROUP // CHANNELS_PER_ATT):
        cells = jnp.where(col_head == head, tall[head * n_cells : (head + 1) * n_cells], cells)
    return cells


def step_kernel(
    n_lat, n_lon, n_blocks, grid_rows, grid_cols,
    targets, tokens, latent, cotangent, inner, outer, projector, sharpness, mixing,
    analysis, in_sum, out_sum,
    latents, cots, cots_above, cots_below, band, outer_t,
    query_rows, query_cols, grad_rows, grad_cols, self_rows,
    features, hidden, slope, block_stats, stats, tile_stats,
    update, update_out, update_in, state, side, rims_out, rims_in, padded, total,
    lat_send, lat_recv, cot_send, cot_recv, rim_send, rim_recv,
    stat_send, stat_recv, up_send, up_recv, halo_send, halo_recv,
    *sum_refs,
):
    lat, lon, mem = (lax.axis_index(name) for name in ("lat", "lon", "mem"))
    n_cells, width = latent.shape
    grads = update
    n_tokens = tokens.shape[0]
    block_len = n_tokens // n_blocks
    groups = width // GROUP
    above, below = lax.rem(lat + n_lat - 1, n_lat), lax.rem(lat + 1, n_lat)
    keep_above = jnp.where(lat > 0, 1.0, 0.0)
    keep_below = jnp.where(lat < n_lat - 1, 1.0, 0.0)
    sectors = [lax.rem(lon + step, n_lon) for step in range(n_lon)]

    partners = [(lat, lon, 1 - mem)]
    partners += [(lat, sector, mem) for sector in sectors[1:]]
    partners += [(row, sector, mem) for row in (above, below) for sector in sectors]
    partners += [(lax.rem(lat + step, n_lat), lon, mem) for step in range(2, n_lat - 1)]
    greet(partners)

    def send(src, dst, send_sem, recv_sem, device):
        copy = pltpu.make_async_remote_copy(
            src_ref=src, dst_ref=dst, send_sem=send_sem, recv_sem=recv_sem,
            device_id=device, device_id_type=MESH)
        copy.start()
        return copy

    arriving = []
    for step in range(1, n_lon):
        arriving.append(send(latent, latents.at[lon], lat_send.at[step], lat_recv.at[step],
                             (lat, sectors[step], mem)))
    for step in range(1, n_lon):
        arriving.append(send(cotangent, cots.at[lon], cot_send.at[step], cot_recv.at[step],
                             (lat, sectors[step], mem)))
    for step in range(n_lon):
        arriving.append(send(cotangent.at[pl.ds(n_cells - 16, 16)], cots_above.at[lon],
                             rim_send.at[0, step], rim_recv.at[0, step],
                             (below, sectors[step], mem)))
        arriving.append(send(cotangent.at[pl.ds(0, 16)], cots_below.at[lon],
                             rim_send.at[1, step], rim_recv.at[1, step],
                             (above, sectors[step], mem)))
    latents[lon] = latent[...]
    cots[lon] = cotangent[...]
    outer_t[...] = outer[...].astype(jnp.float32).T.astype(jnp.bfloat16)

    def perceptron(index, carry):
        rows = rows_of(index, CHUNK)
        pre_act = dot(tokens[rows, :], inner[...])
        sigmoid_val = jax.nn.sigmoid(pre_act)
        slope[rows, :] = sigmoid_val * (1.0 + pre_act * (1.0 - sigmoid_val))
        hidden_act = (pre_act * sigmoid_val).astype(jnp.bfloat16)
        hidden[rows, :] = hidden_act
        features[rows, :] = dot(hidden_act, outer[...]).astype(jnp.bfloat16)
        return carry

    lax.fori_loop(0, n_tokens // CHUNK, perceptron, 0)
    for copy in arriving:
        copy.wait()

    for tile in range(n_lon):
        cols = slice(tile * grid_cols, (tile + 1) * grid_cols)
        band[1 : 1 + grid_rows, cols, :] = (
            cots[tile].astype(jnp.float32).reshape(grid_rows, grid_cols, width))
        band[0, cols, :] = cots_above[tile].astype(jnp.float32)[16 - grid_cols :] * keep_above
        band[1 + grid_rows, cols, :] = cots_below[tile].astype(jnp.float32)[:grid_cols] * keep_below

    def mix_row(row, carry):
        for group in range(groups):
            lanes = lanes_of(group)
            mixed = band[1 + row, :, lanes]
            for index, (row_step, col_step) in enumerate(NEIGHBOURS):
                line = band[1 + row - row_step, :, lanes]
                if col_step:
                    line = pltpu.roll(line, col_step % (n_lon * grid_cols), 0)
                mixed = mixed + mixing[index : index + 1, lanes] * line
            mixed = mixed.astype(jnp.bfloat16).astype(jnp.float32)
            for tile in range(n_lon):
                grads[tile, rows_of(row, grid_cols), lanes] = (
                    mixed[tile * grid_cols : (tile + 1) * grid_cols])
        return carry

    lax.fori_loop(0, grid_rows, mix_row, 0)

    def prepare(tile, carry):
        query = dot(latents[tile], projector[...]).astype(jnp.bfloat16).astype(jnp.float32)
        for group in range(groups):
            lanes = lanes_of(group)
            cell_t = spread_heads(latents[tile, :, lanes].astype(jnp.float32)).T
            spread = spread_heads(query[:, lanes])
            spread_t = spread.T
            query_rows[tile, group] = spread.astype(jnp.bfloat16)
            query_cols[tile, group] = spread_t.astype(jnp.bfloat16)
            self_rows[tile, 0:1, lanes] = (
                jnp.sum(spread_t * cell_t, axis=0, keepdims=True) * sharpness[:, lanes])
            spread = spread_heads(grads[tile, :, lanes])
            spread_t = spread.T
            grad_rows[tile, group] = spread.astype(jnp.bfloat16)
            grad_cols[tile, group] = spread_t.astype(jnp.bfloat16)
            self_rows[tile, 1:2, lanes] = jnp.sum(spread_t * cell_t, axis=0, keepdims=True)
        return carry

    lax.fori_loop(0, n_lon, prepare, 0)

    def block_sums(block, carry):
        tile = targets[block]
        rows = rows_of(block, block_len)
        for group in range(groups):
            lanes = lanes_of(group)
            feature = features[rows, lanes]
            scores = dot(feature, query_cols[tile, group]) * sharpness[:, lanes]
            weight_grad = dot(feature, grad_cols[tile, group])
            top = jnp.max(scores, axis=0, keepdims=True)
            exp_terms = jnp.exp(scores - top)
            block_stats[block, 0:1, lanes] = top
            block_stats[block, 1:2, lanes] = jnp.sum(exp_terms, axis=0, keepdims=True)
            block_stats[block, 2:3, lanes] = jnp.sum(
                exp_terms * weight_grad, axis=0, keepdims=True)
        return carry

    lax.fori_loop(0, n_blocks, block_sums, 0)

    for tile in range(n_lon):
        tops = [jnp.where(targets[block] == tile, block_stats[block, 0:1, :], LOWEST)
                for block in range(n_blocks)]
        top = functools.reduce(jnp.maximum, tops)
        exp_sum = jnp.zeros_like(top)
        grad_sum = jnp.zeros_like(top)
        for block in range(n_blocks):
            scale = jnp.exp(tops[block] - top)
            scale = jnp.where(targets[block] == tile, scale, 0.0)
            exp_sum = exp_sum + scale * block_stats[block, 1:2, :]
            grad_sum = grad_sum + scale * block_stats[block, 2:3, :]
        stats[lon, 4 * tile : 4 * tile + 1, :] = top
        stats[lon, 4 * tile + 1 : 4 * tile + 2, :] = exp_sum
        stats[lon, 4 * tile + 2 : 4 * tile + 3, :] = grad_sum
        stats[lon, 4 * tile + 3 : 4 * tile + 4, :] = jnp.zeros_like(top)

    arriving = [
        send(stats.at[lon], stats.at[lon], stat_send.at[step], stat_recv.at[step],
             (lat, sectors[step], mem))
        for step in range(1, n_lon)]
    update[...] = jnp.zeros_like(update)
    total[...] = jnp.zeros_like(total)
    for copy in arriving:
        copy.wait()

    for tile in range(n_lon):
        self_score = self_rows[tile, 0:1, :]
        top = self_score
        for sector in range(n_lon):
            top = jnp.maximum(top, stats[sector, 4 * tile : 4 * tile + 1, :])
        self_exp = jnp.exp(self_score - top)
        exp_sum = self_exp
        grad_sum = self_exp * self_rows[tile, 1:2, :]
        for sector in range(n_lon):
            scale = jnp.exp(stats[sector, 4 * tile : 4 * tile + 1, :] - top)
            exp_sum = exp_sum + scale * stats[sector, 4 * tile + 1 : 4 * tile + 2, :]
            grad_sum = grad_sum + scale * stats[sector, 4 * tile + 2 : 4 * tile + 3, :]
        inverse = 1.0 / exp_sum
        tile_stats[tile, 0:1, :] = top
        tile_stats[tile, 1:2, :] = inverse
        tile_stats[tile, 2:3, :] = grad_sum * inverse
        tile_stats[tile, 3:4, :] = self_exp * inverse

    def attend(block, carry):
        tile = targets[block]
        rows = rows_of(block, block_len)
        for group in range(groups):
            lanes = lanes_of(group)
            feature = features[rows, lanes]
            scores = dot(feature, query_cols[tile, group]) * sharpness[:, lanes]
            weight_grad = dot(feature, grad_cols[tile, group])
            tile_rows = tile_stats[tile, :, lanes]
            probs = jnp.exp(scores - tile_rows[0:1]) * tile_rows[1:2]
            weights = probs.astype(jnp.bfloat16)
            logit_grad = (
                probs * (weight_grad - tile_rows[2:3]) * sharpness[:, lanes]
            ).astype(jnp.bfloat16)
            features[rows, lanes] = (
                dot(weights, grad_rows[tile, group]) + dot(logit_grad, query_rows[tile, group])
            ).astype(jnp.bfloat16)
            part = gather_heads(dot_rows(weights, feature), n_cells)
            for sector in range(n_lon):
                update[sector, :, lanes] += jnp.where(tile == sector, part, 0.0)
        return carry

    lax.fori_loop(0, n_blocks, attend, 0)

    update_out[...] = update[...].astype(jnp.bfloat16)
    arriving = [
        send(update_out.at[sectors[step]], update_in.at[step], up_send.at[step], up_recv.at[step],
             (lat, sectors[step], mem))
        for step in range(1, n_lon)]

    def perceptron_grad(index, carry):
        rows = rows_of(index, CHUNK)
        feature_grad = features[rows, :]
        hidden_grad = (dot(feature_grad, outer_t[...]) * slope[rows, :]).astype(jnp.bfloat16)
        out_grad = dot_rows(hidden[rows, :], feature_grad)
        total[:GROUP, :GROUP] += dot_rows(tokens[rows, :], hidden_grad)
        total[:GROUP, GROUP:] += out_grad[:, :GROUP]
        total[GROUP:, :] += out_grad[:, GROUP:]
        return carry

    lax.fori_loop(0, n_tokens // CHUNK, perceptron_grad, 0)

    for copy in arriving:
        copy.wait()
    own_stats = tile_stats[lon]
    for group in range(groups):
        lanes = lanes_of(group)
        cells = latent[:, lanes].astype(jnp.float32)
        eye_shape = (GROUP, GROUP)
        eye = lax.broadcasted_iota(jnp.int32, eye_shape, 0) == lax.broadcasted_iota(
            jnp.int32, eye_shape, 1)
        self_weight = own_stats[3:4, lanes].astype(jnp.bfloat16).astype(jnp.float32)
        diagonal = jnp.where(eye, self_weight, 0.0).astype(jnp.bfloat16)
        own = dot(diagonal, spread_heads(cells).astype(jnp.bfloat16))
        change = update[lon, :, lanes] + gather_heads(own, n_cells)
        for step in range(1, n_lon):
            change = change + update_in[step, :, lanes].astype(jnp.float32)
        rounded = (cells + change).astype(jnp.bfloat16).astype(jnp.float32)
        state[:, :, lanes] = rounded.reshape(grid_rows, grid_cols, GROUP)
    for row in range(grid_rows):
        side[row : row + 1, :] = state[row, grid_cols - 1 : grid_cols, :]
        side[grid_rows + row : grid_rows + row + 1, :] = state[row, 0:1, :]
    rims_out[0] = state[0:2].reshape(16, width).astype(jnp.bfloat16)
    rims_out[1] = side[...].astype(jnp.bfloat16)
    rims_out[2] = state[grid_rows - 2 : grid_rows].reshape(16, width).astype(jnp.bfloat16)
    halos = []
    for index, (row_step, col_step) in enumerate(NEIGHBOURS):
        device = ((above, lat, below)[row_step + 1], lax.rem(lon + n_lon + col_step, n_lon), mem)
        halos.append(send(rims_out.at[row_step + 1], rims_in.at[index],
                          halo_send.at[index], halo_recv.at[index], device))

    whole = sum_over_devices(total, n_lat, n_lon, sum_refs)
    in_sum[...] = whole[0, :, :GROUP].astype(jnp.float32)
    out_sum[:, :GROUP] = whole[0, :, GROUP:].astype(jnp.float32)
    out_sum[:, GROUP:] = whole[1].astype(jnp.float32)

    for copy in halos:
        copy.wait()
    first, last = 8, 8 + grid_cols
    padded[1 : 1 + grid_rows, first:last, :] = state[...]
    for index, (row_step, col_step) in enumerate(NEIGHBOURS):
        rim = rims_in[index].astype(jnp.float32)
        if row_step == 0:
            place = first - 1 if col_step == 1 else last
            start = 0 if col_step == 1 else grid_rows
            for row in range(grid_rows):
                padded[1 + row, place : place + 1, :] = rim[start + row : start + row + 1]
        else:
            line = rim[16 - grid_cols :] * keep_above if row_step == 1 else rim[:grid_cols] * keep_below
            place = 0 if row_step == 1 else 1 + grid_rows
            if col_step == 0:
                padded[place, first:last, :] = line
            elif col_step == 1:
                padded[place, first - 1 : first, :] = line[grid_cols - 1 :]
            else:
                padded[place, last : last + 1, :] = line[:1]
    for group in range(groups):
        lanes = lanes_of(group)
        mixed = padded[1 : 1 + grid_rows, first:last, lanes]
        for index, (row_step, col_step) in enumerate(NEIGHBOURS):
            mixed = mixed + mixing[index : index + 1, lanes] * padded[
                1 + row_step : 1 + row_step + grid_rows, first + col_step : last + col_step, lanes]
        analysis[:, lanes] = mixed.reshape(n_cells, GROUP).astype(jnp.bfloat16)


def per_device(
    measured_inputs,
    target_sector,
    hidden_member_fields,
    analysis_adjoint,
    inner_perceptron_coeffs,
    outer_perceptron_coeffs,
    probe_projector,
    logit_sharpness,
    adjacent_channel_coeffs,
):
    n_lat, n_lon = lax.axis_size("lat"), lax.axis_size("lon")
    n_blocks, block_len, obs_width = measured_inputs.shape
    grid_rows, grid_cols, width = hidden_member_fields.shape[1:]
    hidden_width = inner_perceptron_coeffs.shape[1]
    n_cells = grid_rows * grid_cols
    n_tokens = n_blocks * block_len
    groups = width // GROUP
    sharpness = jnp.repeat(logit_sharpness / math.sqrt(CHANNELS_PER_ATT), CHANNELS_PER_ATT)
    bf16, f32 = jnp.bfloat16, jnp.float32
    vmem, dma = pltpu.VMEM, pltpu.SemaphoreType.DMA
    in_vmem = pl.BlockSpec(memory_space=pltpu.VMEM)
    spread = vmem((n_lon, groups, GROUP, GROUP), bf16)
    scratch = [
        vmem((n_lon, n_cells, width), bf16),
        vmem((n_lon, n_cells, width), bf16),
        vmem((n_lon, 16, width), bf16),
        vmem((n_lon, 16, width), bf16),
        vmem((grid_rows + 2, n_lon * grid_cols, width), f32),
        vmem((width, hidden_width), bf16),
        spread, spread, spread, spread,
        vmem((n_lon, 8, width), f32),
        vmem((n_tokens, width), bf16),
        vmem((n_tokens, hidden_width), bf16),
        vmem((n_tokens, hidden_width), f32),
        vmem((n_blocks, 8, width), f32),
        vmem((n_lon, 4 * n_lon, width), f32),
        vmem((n_lon, 8, width), f32),
        vmem((n_lon, n_cells, width), f32),
        vmem((n_lon, n_cells, width), bf16),
        vmem((n_lon, n_cells, width), bf16),
        vmem((grid_rows, grid_cols, width), f32),
        vmem((16, width), f32),
        vmem((3, 16, width), bf16),
        vmem((8, 16, width), bf16),
        vmem((grid_rows + 2, 24, width), f32),
        vmem((2 * GROUP, 2 * GROUP), f32),
        dma((n_lon,)), dma((n_lon,)), dma((n_lon,)), dma((n_lon,)),
        dma((2, n_lon)), dma((2, n_lon)),
        dma((n_lon,)), dma((n_lon,)), dma((n_lon,)), dma((n_lon,)),
        dma((8,)), dma((8,)),
    ] + sum_scratch(n_lat, n_lon, 2 * GROUP, 2 * GROUP)
    analysis, in_grad, out_grad = pl.pallas_call(
        functools.partial(step_kernel, n_lat, n_lon, n_blocks, grid_rows, grid_cols),
        out_shape=[
            jax.ShapeDtypeStruct((n_cells, width), bf16),
            jax.ShapeDtypeStruct(inner_perceptron_coeffs.shape, f32),
            jax.ShapeDtypeStruct(outer_perceptron_coeffs.shape, f32),
        ],
        in_specs=[pl.BlockSpec(memory_space=pltpu.SMEM)] + [in_vmem] * 8,
        out_specs=[in_vmem] * 3,
        scratch_shapes=scratch,
        compiler_params=pltpu.CompilerParams(
            collective_id=0, has_side_effects=True, vmem_limit_bytes=60 << 20
        ),
        name="assimilation_step",
    )(
        target_sector,
        measured_inputs.reshape(n_tokens, obs_width),
        hidden_member_fields.reshape(n_cells, width),
        analysis_adjoint.reshape(n_cells, width),
        inner_perceptron_coeffs,
        outer_perceptron_coeffs,
        probe_projector,
        sharpness[None, :],
        adjacent_channel_coeffs,
    )
    return (analysis.reshape(hidden_member_fields.shape), in_grad, out_grad)


def solution(mesh):
    in_specs = (
        P(("lat", "lon", "mem"), None, None),
        P(("lat", "lon", "mem")),
        P("mem", "lat", "lon", None),
        P("mem", "lat", "lon", None),
        P(),
        P(),
        P(),
        P(),
        P(),
    )
    out_specs = (P("mem", "lat", "lon", None), P(), P())
    return jax.shard_map(
        per_device, mesh=mesh, in_specs=in_specs, out_specs=out_specs, check_vma=False
    )
```

```python
import functools
import math

import jax
import jax.numpy as jnp
from jax import lax
from jax.experimental import pallas as pl
from jax.experimental.pallas import tpu as pltpu
from jax.sharding import PartitionSpec as P

HEADS = 12
CHANNELS_PER_ATT = 64
GROUP = 256
CHUNK = 512
LOWEST = -1e30


NEIGHBOURS = ((-1, -1), (-1, 0), (-1, 1), (0, -1), (0, 1), (1, -1), (1, 0), (1, 1))

MESH = pl.DeviceIdType.MESH


def sum_scratch(n_lat, n_lon, rows, width):
    half = rows // 2
    part = half // n_lon
    return [
        pltpu.VMEM((rows, width), jnp.bfloat16),
        pltpu.VMEM((half, width), jnp.bfloat16),
        pltpu.VMEM((half, width), jnp.float32),
        pltpu.VMEM((n_lon, part, width), jnp.bfloat16),
        pltpu.VMEM((n_lon, part, width), jnp.bfloat16),
        pltpu.VMEM((n_lat, part, width), jnp.bfloat16),
        pltpu.VMEM((2, half, width), jnp.bfloat16),
        pltpu.SemaphoreType.DMA((2,)),
        pltpu.SemaphoreType.DMA((2,)),
        pltpu.SemaphoreType.DMA((2, n_lon)),
        pltpu.SemaphoreType.DMA((2, n_lon)),
        pltpu.SemaphoreType.DMA((n_lat,)),
        pltpu.SemaphoreType.DMA((n_lat,)),
    ]


def sum_over_devices(total, n_lat, n_lon, scratch):
    (rounded, from_core, half_sum, to_lon, from_lon, by_lat, whole,
     core_send, core_recv, lon_send, lon_recv, lat_send, lat_recv) = scratch
    lat, lon, mem = (lax.axis_index(name) for name in ("lat", "lon", "mem"))
    other = 1 - mem
    rows = total.shape[0]
    half = rows // 2
    part = half // n_lon

    rounded[...] = total[...].astype(jnp.bfloat16)
    away = pl.ds(pl.multiple_of(other * half, half), half)
    copy = pltpu.make_async_remote_copy(
        src_ref=rounded.at[away], dst_ref=from_core,
        send_sem=core_send.at[0], recv_sem=core_recv.at[0],
        device_id=(lat, lon, other), device_id_type=MESH)
    copy.start()
    copy.wait()
    mine = pl.ds(pl.multiple_of(mem * half, half), half)
    half_sum[...] = total[mine, :] + from_core[...].astype(jnp.float32)

    to_lon[...] = half_sum[...].astype(jnp.bfloat16).reshape(to_lon.shape)
    copies = []
    for step in range(1, n_lon):
        peer = lax.rem(lon + step, n_lon)
        copy = pltpu.make_async_remote_copy(
            src_ref=to_lon.at[peer], dst_ref=from_lon.at[step],
            send_sem=lon_send.at[0, step], recv_sem=lon_recv.at[0, step],
            device_id=(lat, peer, mem), device_id_type=MESH)
        copy.start()
        copies.append(copy)
    part_sum = half_sum[pl.ds(pl.multiple_of(lon * part, part), part), :]
    for step, copy in enumerate(copies, 1):
        copy.wait()
        part_sum = part_sum + from_lon[step].astype(jnp.float32)

    by_lat[lat] = part_sum.astype(jnp.bfloat16)
    copies = []
    for step in range(1, n_lat):
        peer = lax.rem(lat + step, n_lat)
        copy = pltpu.make_async_remote_copy(
            src_ref=by_lat.at[lat], dst_ref=by_lat.at[lat],
            send_sem=lat_send.at[step], recv_sem=lat_recv.at[step],
            device_id=(peer, lon, mem), device_id_type=MESH)
        copy.start()
        copies.append(copy)
    for copy in copies:
        copy.wait()
    band_sum = by_lat[0].astype(jnp.float32)
    for index in range(1, n_lat):
        band_sum = band_sum + by_lat[index].astype(jnp.float32)

    own = pl.ds(pl.multiple_of(lon * part, part), part)
    whole[mem, own, :] = band_sum.astype(jnp.bfloat16)
    copies = []
    for step in range(1, n_lon):
        peer = lax.rem(lon + step, n_lon)
        copy = pltpu.make_async_remote_copy(
            src_ref=whole.at[mem, own], dst_ref=whole.at[mem, own],
            send_sem=lon_send.at[1, step], recv_sem=lon_recv.at[1, step],
            device_id=(lat, peer, mem), device_id_type=MESH)
        copy.start()
        copies.append(copy)
    for copy in copies:
        copy.wait()
    copy = pltpu.make_async_remote_copy(
        src_ref=whole.at[mem], dst_ref=whole.at[mem],
        send_sem=core_send.at[1], recv_sem=core_recv.at[1],
        device_id=(lat, lon, other), device_id_type=MESH)
    copy.start()
    copy.wait()
    return whole


def greet(partners):
    barrier = pltpu.get_barrier_semaphore()
    for partner in partners:
        pl.semaphore_signal(barrier, inc=1, device_id=partner, device_id_type=MESH)
    pl.semaphore_wait(barrier, len(partners))


def rows_of(index, size):
    return pl.ds(pl.multiple_of(index * size, size), size)


def lanes_of(group):
    return slice(group * GROUP, (group + 1) * GROUP)


def dot(left, right):
    return jnp.dot(left, right, preferred_element_type=jnp.float32)


def dot_rows(left, right):
    return lax.dot_general(
        left, right, (((0,), (0,)), ((), ())), preferred_element_type=jnp.float32
    )


def spread_heads(cells):
    tall = jnp.concatenate([cells] * (GROUP // CHANNELS_PER_ATT), axis=0)
    row_head = lax.broadcasted_iota(jnp.int32, tall.shape, 0) // cells.shape[0]
    col_head = lax.broadcasted_iota(jnp.int32, tall.shape, 1) // CHANNELS_PER_ATT
    return jnp.where(row_head == col_head, tall, 0.0)


def spread_heads_t(cells):
    n_cells = cells.shape[0]
    twice = jnp.concatenate([cells, cells], axis=0).T
    wide = jnp.concatenate([twice] * (GROUP // CHANNELS_PER_ATT // 2), axis=1)
    row_head = lax.broadcasted_iota(jnp.int32, wide.shape, 0) // CHANNELS_PER_ATT
    col_head = lax.broadcasted_iota(jnp.int32, wide.shape, 1) // n_cells
    return jnp.where(row_head == col_head, wide, 0.0)


def gather_heads(tall, n_cells):
    col_head = lax.broadcasted_iota(jnp.int32, (n_cells, GROUP), 1) // CHANNELS_PER_ATT
    cells = tall[:n_cells]
    for head in range(1, GROUP // CHANNELS_PER_ATT):
        cells = jnp.where(col_head == head, tall[head * n_cells : (head + 1) * n_cells], cells)
    return cells


def step_kernel(
    n_lat, n_lon, n_blocks, grid_rows, grid_cols, roomy,
    targets, head_sharpness, tokens, latent, cotangent, inner, outer, projector, mixing,
    analysis, sums,
    latents, cots, cots_above, cots_below, band, outer_t,
    query_rows, query_cols, grad_rows, grad_cols, self_rows,
    features, kept, kept_scores, kept_grads, sharpness, hidden, slope, block_stats, stats, tile_stats,
    update, update_out, update_in, state, side, rims_out, rims_in, padded, total,
    lat_send, lat_recv, cot_send, cot_recv, rim_send, rim_recv,
    stat_send, stat_recv, up_send, up_recv, halo_send, halo_recv,
    *sum_refs,
):
    lat, lon, mem = (lax.axis_index(name) for name in ("lat", "lon", "mem"))
    n_cells, width = latent.shape
    feature_grads = kept if roomy else features
    grads = update
    n_tokens = tokens.shape[0]
    block_len = n_tokens // n_blocks
    groups = width // GROUP
    above, below = lax.rem(lat + n_lat - 1, n_lat), lax.rem(lat + 1, n_lat)
    keep_above = jnp.where(lat > 0, 1.0, 0.0)
    keep_below = jnp.where(lat < n_lat - 1, 1.0, 0.0)
    sectors = [lax.rem(lon + step, n_lon) for step in range(n_lon)]

    partners = [(lat, lon, 1 - mem)]
    partners += [(lat, sector, mem) for sector in sectors[1:]]
    partners += [(row, sector, mem) for row in (above, below) for sector in sectors]
    partners += [(lax.rem(lat + step, n_lat), lon, mem) for step in range(2, n_lat - 1)]
    greet(partners)

    def send(src, dst, send_sem, recv_sem, device):
        copy = pltpu.make_async_remote_copy(
            src_ref=src, dst_ref=dst, send_sem=send_sem, recv_sem=recv_sem,
            device_id=device, device_id_type=MESH)
        copy.start()
        return copy

    arriving = []
    for step in range(1, n_lon):
        arriving.append(send(latent, latents.at[lon], lat_send.at[step], lat_recv.at[step],
                             (lat, sectors[step], mem)))
    for step in range(1, n_lon):
        arriving.append(send(cotangent, cots.at[lon], cot_send.at[step], cot_recv.at[step],
                             (lat, sectors[step], mem)))
    for step in range(n_lon):
        arriving.append(send(cotangent.at[pl.ds(n_cells - 16, 16)], cots_above.at[lon],
                             rim_send.at[0, step], rim_recv.at[0, step],
                             (below, sectors[step], mem)))
        arriving.append(send(cotangent.at[pl.ds(0, 16)], cots_below.at[lon],
                             rim_send.at[1, step], rim_recv.at[1, step],
                             (above, sectors[step], mem)))
    head = lax.broadcasted_iota(jnp.int32, (1, width), 1) // CHANNELS_PER_ATT
    row = jnp.zeros((1, width), jnp.float32)
    for index in range(HEADS):
        row = jnp.where(head == index, head_sharpness[index], row)
    sharpness[...] = row / math.sqrt(CHANNELS_PER_ATT)
    latents[lon] = latent[...]
    cots[lon] = cotangent[...]
    outer_t[...] = outer[...].astype(jnp.float32).T.astype(jnp.bfloat16)

    def perceptron(index, carry):
        rows = rows_of(index, CHUNK)
        pre_act = dot(tokens[rows, :], inner[...])
        sigmoid_val = jax.nn.sigmoid(pre_act)
        slope[rows, :] = sigmoid_val * (1.0 + pre_act * (1.0 - sigmoid_val))
        hidden_act = (pre_act * sigmoid_val).astype(jnp.bfloat16)
        hidden[rows, :] = hidden_act
        features[rows, :] = dot(hidden_act, outer[...]).astype(jnp.bfloat16)
        return carry

    lax.fori_loop(0, n_tokens // CHUNK, perceptron, 0)
    for copy in arriving[: n_lon - 1]:
        copy.wait()

    def prepare_queries(tile, carry):
        query = dot(latents[tile], projector[...]).astype(jnp.bfloat16).astype(jnp.float32)
        for group in range(groups):
            lanes = lanes_of(group)
            cell_t = spread_heads_t(latents[tile, :, lanes].astype(jnp.float32))
            spread_t = spread_heads_t(query[:, lanes])
            query_rows[tile, group] = spread_heads(query[:, lanes]).astype(jnp.bfloat16)
            query_cols[tile, group] = spread_t.astype(jnp.bfloat16)
            self_rows[tile, 0:1, lanes] = (
                jnp.sum(spread_t * cell_t, axis=0, keepdims=True) * sharpness[:, lanes])
        return carry

    lax.fori_loop(0, n_lon, prepare_queries, 0)
    for copy in arriving[n_lon - 1 :]:
        copy.wait()

    for tile in range(n_lon):
        cols = slice(tile * grid_cols, (tile + 1) * grid_cols)
        band[1 : 1 + grid_rows, cols, :] = (
            cots[tile].astype(jnp.float32).reshape(grid_rows, grid_cols, width))
        band[0, cols, :] = cots_above[tile].astype(jnp.float32)[16 - grid_cols :] * keep_above
        band[1 + grid_rows, cols, :] = cots_below[tile].astype(jnp.float32)[:grid_cols] * keep_below

    def mix_row(row, carry):
        for group in range(groups):
            lanes = lanes_of(group)
            mixed = band[1 + row, :, lanes]
            for index, (row_step, col_step) in enumerate(NEIGHBOURS):
                line = band[1 + row - row_step, :, lanes]
                if col_step:
                    line = pltpu.roll(line, col_step % (n_lon * grid_cols), 0)
                mixed = mixed + mixing[index : index + 1, lanes] * line
            mixed = mixed.astype(jnp.bfloat16).astype(jnp.float32)
            for tile in range(n_lon):
                grads[tile, rows_of(row, grid_cols), lanes] = (
                    mixed[tile * grid_cols : (tile + 1) * grid_cols])
        return carry

    lax.fori_loop(0, grid_rows, mix_row, 0)

    def prepare_grads(tile, carry):
        for group in range(groups):
            lanes = lanes_of(group)
            cell_t = spread_heads_t(latents[tile, :, lanes].astype(jnp.float32))
            spread_t = spread_heads_t(grads[tile, :, lanes])
            grad_rows[tile, group] = spread_heads(grads[tile, :, lanes]).astype(jnp.bfloat16)
            grad_cols[tile, group] = spread_t.astype(jnp.bfloat16)
            self_rows[tile, 1:2, lanes] = jnp.sum(spread_t * cell_t, axis=0, keepdims=True)
        return carry

    lax.fori_loop(0, n_lon, prepare_grads, 0)

    def block_sums(pair, carry):
        for block, group in [(2 * pair + i, j) for i in range(2) for j in range(groups)]:
            tile = targets[block]
            rows = rows_of(block, block_len)
            lanes = lanes_of(group)
            feature = features[rows, lanes]
            scores = dot(feature, query_cols[tile, group]) * sharpness[:, lanes]
            weight_grad = dot(feature, grad_cols[tile, group])
            if roomy:
                kept_scores[rows, lanes] = scores
                kept_grads[rows, lanes] = weight_grad
            top = jnp.max(scores, axis=0, keepdims=True)
            exp_terms = jnp.exp(scores - top)
            block_stats[block, 0:1, lanes] = top
            block_stats[block, 1:2, lanes] = jnp.sum(exp_terms, axis=0, keepdims=True)
            block_stats[block, 2:3, lanes] = jnp.sum(
                exp_terms * weight_grad, axis=0, keepdims=True)
        return carry

    lax.fori_loop(0, n_blocks // 2, block_sums, 0)

    for tile in range(n_lon):
        tops = [jnp.where(targets[block] == tile, block_stats[block, 0:1, :], LOWEST)
                for block in range(n_blocks)]
        top = functools.reduce(jnp.maximum, tops)
        exp_sum = jnp.zeros_like(top)
        grad_sum = jnp.zeros_like(top)
        for block in range(n_blocks):
            scale = jnp.exp(tops[block] - top)
            scale = jnp.where(targets[block] == tile, scale, 0.0)
            exp_sum = exp_sum + scale * block_stats[block, 1:2, :]
            grad_sum = grad_sum + scale * block_stats[block, 2:3, :]
        stats[lon, 4 * tile : 4 * tile + 1, :] = top
        stats[lon, 4 * tile + 1 : 4 * tile + 2, :] = exp_sum
        stats[lon, 4 * tile + 2 : 4 * tile + 3, :] = grad_sum
        stats[lon, 4 * tile + 3 : 4 * tile + 4, :] = jnp.zeros_like(top)

    arriving = [
        send(stats.at[lon], stats.at[lon], stat_send.at[step], stat_recv.at[step],
             (lat, sectors[step], mem))
        for step in range(1, n_lon)]
    update[...] = jnp.zeros_like(update)
    total[...] = jnp.zeros_like(total)
    for copy in arriving:
        copy.wait()

    for tile in range(n_lon):
        self_score = self_rows[tile, 0:1, :]
        top = self_score
        for sector in range(n_lon):
            top = jnp.maximum(top, stats[sector, 4 * tile : 4 * tile + 1, :])
        self_exp = jnp.exp(self_score - top)
        exp_sum = self_exp
        grad_sum = self_exp * self_rows[tile, 1:2, :]
        for sector in range(n_lon):
            scale = jnp.exp(stats[sector, 4 * tile : 4 * tile + 1, :] - top)
            exp_sum = exp_sum + scale * stats[sector, 4 * tile + 1 : 4 * tile + 2, :]
            grad_sum = grad_sum + scale * stats[sector, 4 * tile + 2 : 4 * tile + 3, :]
        inverse = 1.0 / exp_sum
        tile_stats[tile, 0:1, :] = top
        tile_stats[tile, 1:2, :] = inverse
        tile_stats[tile, 2:3, :] = grad_sum * inverse
        tile_stats[tile, 3:4, :] = self_exp * inverse

    def attend(pair, carry):
        for block, group in [(2 * pair + i, j) for i in range(2) for j in range(groups)]:
            tile = targets[block]
            rows = rows_of(block, block_len)
            lanes = lanes_of(group)
            feature = features[rows, lanes]
            if roomy:
                scores = kept_scores[rows, lanes]
                weight_grad = kept_grads[rows, lanes]
            else:
                scores = dot(feature, query_cols[tile, group]) * sharpness[:, lanes]
                weight_grad = dot(feature, grad_cols[tile, group])
            tile_rows = tile_stats[tile, :, lanes]
            probs = jnp.exp(scores - tile_rows[0:1]) * tile_rows[1:2]
            weights = probs.astype(jnp.bfloat16)
            logit_grad = (
                probs * (weight_grad - tile_rows[2:3]) * sharpness[:, lanes]
            ).astype(jnp.bfloat16)
            feature_grads[rows, lanes] = (
                dot(weights, grad_rows[tile, group]) + dot(logit_grad, query_rows[tile, group])
            ).astype(jnp.bfloat16)
            part = gather_heads(dot_rows(weights, feature), n_cells)
            for sector in range(n_lon):
                update[sector, :, lanes] += jnp.where(tile == sector, part, 0.0)
        return carry

    lax.fori_loop(0, n_blocks // 2, attend, 0)

    update_out[...] = update[...].astype(jnp.bfloat16)
    arriving = [
        send(update_out.at[sectors[step]], update_in.at[step], up_send.at[step], up_recv.at[step],
             (lat, sectors[step], mem))
        for step in range(1, n_lon)]

    def perceptron_grad(index, carry):
        rows = rows_of(index, CHUNK)
        feature_grad = feature_grads[rows, :]
        hidden_grad = (dot(feature_grad, outer_t[...]) * slope[rows, :]).astype(jnp.bfloat16)
        out_grad = dot_rows(hidden[rows, :], feature_grad)
        total[:GROUP, :GROUP] += dot_rows(tokens[rows, :], hidden_grad)
        total[:GROUP, GROUP:] += out_grad[:, :GROUP]
        total[GROUP:, :] += out_grad[:, GROUP:]
        return carry

    lax.fori_loop(0, n_tokens // CHUNK, perceptron_grad, 0)

    for copy in arriving:
        copy.wait()
    own_stats = tile_stats[lon]
    for group in range(groups):
        lanes = lanes_of(group)
        cells = latent[:, lanes].astype(jnp.float32)
        eye_shape = (GROUP, GROUP)
        eye = lax.broadcasted_iota(jnp.int32, eye_shape, 0) == lax.broadcasted_iota(
            jnp.int32, eye_shape, 1)
        self_weight = own_stats[3:4, lanes].astype(jnp.bfloat16).astype(jnp.float32)
        diagonal = jnp.where(eye, self_weight, 0.0).astype(jnp.bfloat16)
        own = dot(diagonal, spread_heads(cells).astype(jnp.bfloat16))
        change = update[lon, :, lanes] + gather_heads(own, n_cells)
        for step in range(1, n_lon):
            change = change + update_in[step, :, lanes].astype(jnp.float32)
        rounded = (cells + change).astype(jnp.bfloat16).astype(jnp.float32)
        state[:, :, lanes] = rounded.reshape(grid_rows, grid_cols, GROUP)
    for row in range(grid_rows):
        side[row : row + 1, :] = state[row, grid_cols - 1 : grid_cols, :]
        side[grid_rows + row : grid_rows + row + 1, :] = state[row, 0:1, :]
    rims_out[0] = state[0:2].reshape(16, width).astype(jnp.bfloat16)
    rims_out[1] = side[...].astype(jnp.bfloat16)
    rims_out[2] = state[grid_rows - 2 : grid_rows].reshape(16, width).astype(jnp.bfloat16)
    halos = []
    for index, (row_step, col_step) in enumerate(NEIGHBOURS):
        device = ((above, lat, below)[row_step + 1], lax.rem(lon + n_lon + col_step, n_lon), mem)
        halos.append(send(rims_out.at[row_step + 1], rims_in.at[index],
                          halo_send.at[index], halo_recv.at[index], device))

    whole = sum_over_devices(total, n_lat, n_lon, sum_refs)
    sums[...] = whole[...]

    for copy in halos:
        copy.wait()
    first, last = 8, 8 + grid_cols
    padded[1 : 1 + grid_rows, first:last, :] = state[...]
    for index, (row_step, col_step) in enumerate(NEIGHBOURS):
        rim = rims_in[index].astype(jnp.float32)
        if row_step == 0:
            place = first - 1 if col_step == 1 else last
            start = 0 if col_step == 1 else grid_rows
            for row in range(grid_rows):
                padded[1 + row, place : place + 1, :] = rim[start + row : start + row + 1]
        else:
            line = rim[16 - grid_cols :] * keep_above if row_step == 1 else rim[:grid_cols] * keep_below
            place = 0 if row_step == 1 else 1 + grid_rows
            if col_step == 0:
                padded[place, first:last, :] = line
            elif col_step == 1:
                padded[place, first - 1 : first, :] = line[grid_cols - 1 :]
            else:
                padded[place, last : last + 1, :] = line[:1]
    for group in range(groups):
        lanes = lanes_of(group)
        mixed = padded[1 : 1 + grid_rows, first:last, lanes]
        for index, (row_step, col_step) in enumerate(NEIGHBOURS):
            mixed = mixed + mixing[index : index + 1, lanes] * padded[
                1 + row_step : 1 + row_step + grid_rows, first + col_step : last + col_step, lanes]
        analysis[:, lanes] = mixed.reshape(n_cells, GROUP).astype(jnp.bfloat16)


def finish_kernel(analysis, sums, analysis_out, in_sum, out_sum):
    analysis_out[...] = analysis[...]
    in_sum[...] = sums[0, :, :GROUP].astype(jnp.float32)
    out_sum[:, :GROUP] = sums[0, :, GROUP:].astype(jnp.float32)
    out_sum[:, GROUP:] = sums[1].astype(jnp.float32)


def per_device(
    measured_inputs,
    target_sector,
    hidden_member_fields,
    analysis_adjoint,
    inner_perceptron_coeffs,
    outer_perceptron_coeffs,
    probe_projector,
    logit_sharpness,
    adjacent_channel_coeffs,
):
    n_lat, n_lon = lax.axis_size("lat"), lax.axis_size("lon")
    n_blocks, block_len, obs_width = measured_inputs.shape
    grid_rows, grid_cols, width = hidden_member_fields.shape[1:]
    hidden_width = inner_perceptron_coeffs.shape[1]
    n_cells = grid_rows * grid_cols
    n_tokens = n_blocks * block_len
    groups = width // GROUP
    roomy = n_lon <= 4
    bf16, f32 = jnp.bfloat16, jnp.float32
    vmem, dma = pltpu.VMEM, pltpu.SemaphoreType.DMA
    in_vmem = pl.BlockSpec(memory_space=pltpu.VMEM)
    spread = vmem((n_lon, groups, GROUP, GROUP), bf16)
    scratch = [
        vmem((n_lon, n_cells, width), bf16),
        vmem((n_lon, n_cells, width), bf16),
        vmem((n_lon, 16, width), bf16),
        vmem((n_lon, 16, width), bf16),
        vmem((grid_rows + 2, n_lon * grid_cols, width), f32),
        vmem((width, hidden_width), bf16),
        spread, spread, spread, spread,
        vmem((n_lon, 8, width), f32),
        vmem((n_tokens, width), bf16),
        vmem((n_tokens if roomy else 16, width), bf16),
        vmem((n_tokens if roomy else 8, width), f32),
        vmem((n_tokens if roomy else 8, width), f32),
        vmem((1, width), f32),
        vmem((n_tokens, hidden_width), bf16),
        vmem((n_tokens, hidden_width), f32),
        vmem((n_blocks, 8, width), f32),
        vmem((n_lon, 4 * n_lon, width), f32),
        vmem((n_lon, 8, width), f32),
        vmem((n_lon, n_cells, width), f32),
        vmem((n_lon, n_cells, width), bf16),
        vmem((n_lon, n_cells, width), bf16),
        vmem((grid_rows, grid_cols, width), f32),
        vmem((16, width), f32),
        vmem((3, 16, width), bf16),
        vmem((8, 16, width), bf16),
        vmem((grid_rows + 2, 24, width), f32),
        vmem((2 * GROUP, 2 * GROUP), f32),
        dma((n_lon,)), dma((n_lon,)), dma((n_lon,)), dma((n_lon,)),
        dma((2, n_lon)), dma((2, n_lon)),
        dma((n_lon,)), dma((n_lon,)), dma((n_lon,)), dma((n_lon,)),
        dma((8,)), dma((8,)),
    ] + sum_scratch(n_lat, n_lon, 2 * GROUP, 2 * GROUP)
    in_smem = pl.BlockSpec(memory_space=pltpu.SMEM)
    analysis, sums = pl.pallas_call(
        functools.partial(step_kernel, n_lat, n_lon, n_blocks, grid_rows, grid_cols, roomy),
        out_shape=[
            jax.ShapeDtypeStruct((n_cells, width), bf16),
            jax.ShapeDtypeStruct((2, GROUP, 2 * GROUP), bf16),
        ],
        in_specs=[in_smem] * 2 + [in_vmem] * 7,
        out_specs=[in_vmem] * 2,
        scratch_shapes=scratch,
        compiler_params=pltpu.CompilerParams(
            collective_id=0, has_side_effects=True, vmem_limit_bytes=60 << 20
        ),
        name="assimilation_step",
    )(
        target_sector,
        logit_sharpness,
        measured_inputs.reshape(n_tokens, obs_width),
        hidden_member_fields.reshape(n_cells, width),
        analysis_adjoint.reshape(n_cells, width),
        inner_perceptron_coeffs,
        outer_perceptron_coeffs,
        probe_projector,
        adjacent_channel_coeffs,
    )
    analysis, in_grad, out_grad = pl.pallas_call(
        finish_kernel,
        out_shape=[
            jax.ShapeDtypeStruct((n_cells, width), bf16),
            jax.ShapeDtypeStruct(inner_perceptron_coeffs.shape, f32),
            jax.ShapeDtypeStruct(outer_perceptron_coeffs.shape, f32),
        ],
        in_specs=[in_vmem] * 2,
        out_specs=[in_vmem] * 3,
        compiler_params=pltpu.CompilerParams(vmem_limit_bytes=16 << 20),
        name="to_float32",
    )(analysis, sums)
    return (analysis.reshape(hidden_member_fields.shape), in_grad, out_grad)


def solution(mesh):
    in_specs = (
        P(("lat", "lon", "mem"), None, None),
        P(("lat", "lon", "mem")),
        P("mem", "lat", "lon", None),
        P("mem", "lat", "lon", None),
        P(),
        P(),
        P(),
        P(),
        P(),
    )
    out_specs = (P("mem", "lat", "lon", None), P(), P())
    return jax.shard_map(
        per_device, mesh=mesh, in_specs=in_specs, out_specs=out_specs, check_vma=False
    )
```

```python
import functools
import math

import jax
import jax.numpy as jnp
from jax import lax
from jax.experimental import pallas as pl
from jax.experimental.pallas import tpu as pltpu
from jax.sharding import PartitionSpec as P

HEADS = 12
CHANNELS_PER_ATT = 64
GROUP = 256
CHUNK = 512
LOWEST = -1e30


NEIGHBOURS = ((-1, -1), (-1, 0), (-1, 1), (0, -1), (0, 1), (1, -1), (1, 0), (1, 1))

MESH = pl.DeviceIdType.MESH
PIECE = 128


def sum_scratch(n_lat, n_lon, pieces, rows):
    peers = 2 * n_lon
    part = rows // peers
    by_peer = pltpu.VMEM((pieces, peers, part, PIECE), jnp.bfloat16)
    return [
        by_peer, by_peer,
        pltpu.VMEM((pieces, n_lat, part, PIECE), jnp.bfloat16),
        by_peer,
        pltpu.SemaphoreType.DMA((pieces, 2, peers)),
        pltpu.SemaphoreType.DMA((pieces, 2, peers)),
        pltpu.SemaphoreType.DMA((pieces, n_lat)),
        pltpu.SemaphoreType.DMA((pieces, n_lat)),
    ]


def sum_piece(piece, total, n_lat, n_lon, scratch):
    rounded, arrived, by_lat, whole, peer_send, peer_recv, lat_send, lat_recv = scratch
    lat, lon, mem = (lax.axis_index(name) for name in ("lat", "lon", "mem"))
    peers = 2 * n_lon
    part = total.shape[1] // peers
    me = 2 * lon + mem

    rounded[piece] = total[piece].astype(jnp.bfloat16).reshape(rounded.shape[1:])
    copies = []
    for step in range(1, peers):
        peer = lax.rem(me + step, peers)
        copies.append(pltpu.make_async_remote_copy(
            src_ref=rounded.at[piece, peer], dst_ref=arrived.at[piece, step],
            send_sem=peer_send.at[piece, 0, step], recv_sem=peer_recv.at[piece, 0, step],
            device_id=(lat, lax.div(peer, 2), lax.rem(peer, 2)), device_id_type=MESH))
        copies[-1].start()
    yield
    part_sum = total[piece, pl.ds(pl.multiple_of(me * part, part), part), :]
    for step, copy in enumerate(copies, 1):
        copy.wait()
        part_sum = part_sum + arrived[piece, step].astype(jnp.float32)

    by_lat[piece, lat] = part_sum.astype(jnp.bfloat16)
    copies = []
    for step in range(1, n_lat):
        copies.append(pltpu.make_async_remote_copy(
            src_ref=by_lat.at[piece, lat], dst_ref=by_lat.at[piece, lat],
            send_sem=lat_send.at[piece, step], recv_sem=lat_recv.at[piece, step],
            device_id=(lax.rem(lat + step, n_lat), lon, mem), device_id_type=MESH))
        copies[-1].start()
    yield
    for copy in copies:
        copy.wait()
    band_sum = by_lat[piece, 0].astype(jnp.float32)
    for index in range(1, n_lat):
        band_sum = band_sum + by_lat[piece, index].astype(jnp.float32)

    whole[piece, me] = band_sum.astype(jnp.bfloat16)
    copies = []
    for step in range(1, peers):
        peer = lax.rem(me + step, peers)
        copies.append(pltpu.make_async_remote_copy(
            src_ref=whole.at[piece, me], dst_ref=whole.at[piece, me],
            send_sem=peer_send.at[piece, 1, step], recv_sem=peer_recv.at[piece, 1, step],
            device_id=(lat, lax.div(peer, 2), lax.rem(peer, 2)), device_id_type=MESH))
        copies[-1].start()
    yield
    for copy in copies:
        copy.wait()
    yield


def greet(partners):
    barrier = pltpu.get_barrier_semaphore()
    for partner in partners:
        pl.semaphore_signal(barrier, inc=1, device_id=partner, device_id_type=MESH)
    pl.semaphore_wait(barrier, len(partners))


def rows_of(index, size):
    return pl.ds(pl.multiple_of(index * size, size), size)


def lanes_of(group):
    return slice(group * GROUP, (group + 1) * GROUP)


def dot(left, right):
    return jnp.dot(left, right, preferred_element_type=jnp.float32)


def dot_rows(left, right):
    return lax.dot_general(
        left, right, (((0,), (0,)), ((), ())), preferred_element_type=jnp.float32
    )


def spread_heads(cells):
    tall = jnp.concatenate([cells] * (GROUP // CHANNELS_PER_ATT), axis=0)
    row_head = lax.broadcasted_iota(jnp.int32, tall.shape, 0) // cells.shape[0]
    col_head = lax.broadcasted_iota(jnp.int32, tall.shape, 1) // CHANNELS_PER_ATT
    return jnp.where(row_head == col_head, tall, 0.0)


def spread_heads_t(cells):
    n_cells = cells.shape[0]
    twice = jnp.concatenate([cells, cells], axis=0).T
    wide = jnp.concatenate([twice] * (GROUP // CHANNELS_PER_ATT // 2), axis=1)
    row_head = lax.broadcasted_iota(jnp.int32, wide.shape, 0) // CHANNELS_PER_ATT
    col_head = lax.broadcasted_iota(jnp.int32, wide.shape, 1) // n_cells
    return jnp.where(row_head == col_head, wide, 0.0)


def gather_heads(tall, n_cells):
    col_head = lax.broadcasted_iota(jnp.int32, (n_cells, GROUP), 1) // CHANNELS_PER_ATT
    cells = tall[:n_cells]
    for head in range(1, GROUP // CHANNELS_PER_ATT):
        cells = jnp.where(col_head == head, tall[head * n_cells : (head + 1) * n_cells], cells)
    return cells


def step_kernel(
    n_lat, n_lon, n_blocks, grid_rows, grid_cols, roomy,
    targets, head_sharpness, tokens, latent, cotangent, inner, outer, projector, mixing,
    analysis, sums,
    latents, cots, cots_above, cots_below, band, outer_t,
    query_rows, query_cols, grad_rows, grad_cols, self_rows,
    features, kept, kept_scores, kept_grads, sharpness, hidden_t, tokens_t, slope, block_stats, stats, tile_stats,
    update, update_out, update_in, state, side, rims_out, rims_in, padded, total,
    lat_send, lat_recv, cot_send, cot_recv, rim_send, rim_recv,
    stat_send, stat_recv, up_send, up_recv, halo_send, halo_recv,
    *sum_refs,
):
    lat, lon, mem = (lax.axis_index(name) for name in ("lat", "lon", "mem"))
    n_cells, width = latent.shape
    feature_grads = kept if roomy else features
    grads = update
    n_tokens = tokens.shape[0]
    block_len = n_tokens // n_blocks
    groups = width // GROUP
    above, below = lax.rem(lat + n_lat - 1, n_lat), lax.rem(lat + 1, n_lat)
    keep_above = jnp.where(lat > 0, 1.0, 0.0)
    keep_below = jnp.where(lat < n_lat - 1, 1.0, 0.0)
    sectors = [lax.rem(lon + step, n_lon) for step in range(n_lon)]

    partners = [(lat, sector, mem) for sector in sectors[1:]]
    partners += [(lat, sector, 1 - mem) for sector in sectors]
    partners += [(row, sector, mem) for row in (above, below) for sector in sectors]
    partners += [(lax.rem(lat + step, n_lat), lon, mem) for step in range(2, n_lat - 1)]
    greet(partners)

    def send(src, dst, send_sem, recv_sem, device):
        copy = pltpu.make_async_remote_copy(
            src_ref=src, dst_ref=dst, send_sem=send_sem, recv_sem=recv_sem,
            device_id=device, device_id_type=MESH)
        copy.start()
        return copy

    arriving = []
    for step in range(1, n_lon):
        arriving.append(send(latent, latents.at[lon], lat_send.at[step], lat_recv.at[step],
                             (lat, sectors[step], mem)))
    for step in range(1, n_lon):
        arriving.append(send(cotangent, cots.at[lon], cot_send.at[step], cot_recv.at[step],
                             (lat, sectors[step], mem)))
    for step in range(n_lon):
        arriving.append(send(cotangent.at[pl.ds(n_cells - 16, 16)], cots_above.at[lon],
                             rim_send.at[0, step], rim_recv.at[0, step],
                             (below, sectors[step], mem)))
        arriving.append(send(cotangent.at[pl.ds(0, 16)], cots_below.at[lon],
                             rim_send.at[1, step], rim_recv.at[1, step],
                             (above, sectors[step], mem)))
    head = lax.broadcasted_iota(jnp.int32, (1, width), 1) // CHANNELS_PER_ATT
    row = jnp.zeros((1, width), jnp.float32)
    for index in range(HEADS):
        row = jnp.where(head == index, head_sharpness[index], row)
    sharpness[...] = row / math.sqrt(CHANNELS_PER_ATT)
    latents[lon] = latent[...]
    cots[lon] = cotangent[...]
    outer_t[...] = outer[...].astype(jnp.float32).T.astype(jnp.bfloat16)

    def perceptron(index, carry):
        rows = rows_of(index, CHUNK)
        pre_act = dot(tokens[rows, :], inner[...])
        sigmoid_val = jax.nn.sigmoid(pre_act)
        slope[rows, :] = sigmoid_val * (1.0 + pre_act * (1.0 - sigmoid_val))
        hidden_act = (pre_act * sigmoid_val).astype(jnp.bfloat16)
        hidden_t[:, rows] = hidden_act.T
        tokens_t[:, rows] = tokens[rows, :].T
        features[rows, :] = dot(hidden_act, outer[...]).astype(jnp.bfloat16)
        return carry

    lax.fori_loop(0, n_tokens // CHUNK, perceptron, 0)
    for copy in arriving[: n_lon - 1]:
        copy.wait()

    def prepare_queries(tile, carry):
        query = dot(latents[tile], projector[...]).astype(jnp.bfloat16).astype(jnp.float32)
        for group in range(groups):
            lanes = lanes_of(group)
            cell_t = spread_heads_t(latents[tile, :, lanes].astype(jnp.float32))
            spread_t = spread_heads_t(query[:, lanes])
            query_rows[tile, group] = spread_heads(query[:, lanes]).astype(jnp.bfloat16)
            query_cols[tile, group] = spread_t.astype(jnp.bfloat16)
            self_rows[tile, 0:1, lanes] = (
                jnp.sum(spread_t * cell_t, axis=0, keepdims=True) * sharpness[:, lanes])
        return carry

    lax.fori_loop(0, n_lon, prepare_queries, 0)
    for copy in arriving[n_lon - 1 :]:
        copy.wait()

    for tile in range(n_lon):
        cols = slice(tile * grid_cols, (tile + 1) * grid_cols)
        band[1 : 1 + grid_rows, cols, :] = (
            cots[tile].astype(jnp.float32).reshape(grid_rows, grid_cols, width))
        band[0, cols, :] = cots_above[tile].astype(jnp.float32)[16 - grid_cols :] * keep_above
        band[1 + grid_rows, cols, :] = cots_below[tile].astype(jnp.float32)[:grid_cols] * keep_below

    def mix_row(row, carry):
        for group in range(groups):
            lanes = lanes_of(group)
            mixed = band[1 + row, :, lanes]
            for index, (row_step, col_step) in enumerate(NEIGHBOURS):
                line = band[1 + row - row_step, :, lanes]
                if col_step:
                    line = pltpu.roll(line, col_step % (n_lon * grid_cols), 0)
                mixed = mixed + mixing[index : index + 1, lanes] * line
            mixed = mixed.astype(jnp.bfloat16).astype(jnp.float32)
            for tile in range(n_lon):
                grads[tile, rows_of(row, grid_cols), lanes] = (
                    mixed[tile * grid_cols : (tile + 1) * grid_cols])
        return carry

    lax.fori_loop(0, grid_rows, mix_row, 0)

    def prepare_grads(tile, carry):
        for group in range(groups):
            lanes = lanes_of(group)
            cell_t = spread_heads_t(latents[tile, :, lanes].astype(jnp.float32))
            spread_t = spread_heads_t(grads[tile, :, lanes])
            grad_rows[tile, group] = spread_heads(grads[tile, :, lanes]).astype(jnp.bfloat16)
            grad_cols[tile, group] = spread_t.astype(jnp.bfloat16)
            self_rows[tile, 1:2, lanes] = jnp.sum(spread_t * cell_t, axis=0, keepdims=True)
        return carry

    lax.fori_loop(0, n_lon, prepare_grads, 0)

    def block_sums(pair, carry):
        for block, group in [(2 * pair + i, j) for i in range(2) for j in range(groups)]:
            tile = targets[block]
            rows = rows_of(block, block_len)
            lanes = lanes_of(group)
            feature = features[rows, lanes]
            scores = dot(feature, query_cols[tile, group]) * sharpness[:, lanes]
            weight_grad = dot(feature, grad_cols[tile, group])
            if roomy:
                kept_scores[rows, lanes] = scores
                kept_grads[rows, lanes] = weight_grad
            top = jnp.max(scores, axis=0, keepdims=True)
            exp_terms = jnp.exp(scores - top)
            block_stats[block, 0:1, lanes] = top
            block_stats[block, 1:2, lanes] = jnp.sum(exp_terms, axis=0, keepdims=True)
            block_stats[block, 2:3, lanes] = jnp.sum(
                exp_terms * weight_grad, axis=0, keepdims=True)
        return carry

    lax.fori_loop(0, n_blocks // 2, block_sums, 0)

    for tile in range(n_lon):
        tops = [jnp.where(targets[block] == tile, block_stats[block, 0:1, :], LOWEST)
                for block in range(n_blocks)]
        top = functools.reduce(jnp.maximum, tops)
        exp_sum = jnp.zeros_like(top)
        grad_sum = jnp.zeros_like(top)
        for block in range(n_blocks):
            scale = jnp.exp(tops[block] - top)
            scale = jnp.where(targets[block] == tile, scale, 0.0)
            exp_sum = exp_sum + scale * block_stats[block, 1:2, :]
            grad_sum = grad_sum + scale * block_stats[block, 2:3, :]
        stats[lon, 4 * tile : 4 * tile + 1, :] = top
        stats[lon, 4 * tile + 1 : 4 * tile + 2, :] = exp_sum
        stats[lon, 4 * tile + 2 : 4 * tile + 3, :] = grad_sum
        stats[lon, 4 * tile + 3 : 4 * tile + 4, :] = jnp.zeros_like(top)

    arriving = [
        send(stats.at[lon], stats.at[lon], stat_send.at[step], stat_recv.at[step],
             (lat, sectors[step], mem))
        for step in range(1, n_lon)]
    update[...] = jnp.zeros_like(update)
    total[...] = jnp.zeros_like(total)
    for copy in arriving:
        copy.wait()

    for tile in range(n_lon):
        self_score = self_rows[tile, 0:1, :]
        top = self_score
        for sector in range(n_lon):
            top = jnp.maximum(top, stats[sector, 4 * tile : 4 * tile + 1, :])
        self_exp = jnp.exp(self_score - top)
        exp_sum = self_exp
        grad_sum = self_exp * self_rows[tile, 1:2, :]
        for sector in range(n_lon):
            scale = jnp.exp(stats[sector, 4 * tile : 4 * tile + 1, :] - top)
            exp_sum = exp_sum + scale * stats[sector, 4 * tile + 1 : 4 * tile + 2, :]
            grad_sum = grad_sum + scale * stats[sector, 4 * tile + 2 : 4 * tile + 3, :]
        inverse = 1.0 / exp_sum
        tile_stats[tile, 0:1, :] = top
        tile_stats[tile, 1:2, :] = inverse
        tile_stats[tile, 2:3, :] = grad_sum * inverse
        tile_stats[tile, 3:4, :] = self_exp * inverse

    def attend(group, first, last):
        lanes = lanes_of(group)

        def four_blocks(index, carry):
            for block in [4 * index + i for i in range(4)]:
                tile = targets[block]
                rows = rows_of(block, block_len)
                feature = features[rows, lanes]
                if roomy:
                    scores = kept_scores[rows, lanes]
                    weight_grad = kept_grads[rows, lanes]
                else:
                    scores = dot(feature, query_cols[tile, group]) * sharpness[:, lanes]
                    weight_grad = dot(feature, grad_cols[tile, group])
                tile_rows = tile_stats[tile, :, lanes]
                probs = jnp.exp(scores - tile_rows[0:1]) * tile_rows[1:2]
                weights = probs.astype(jnp.bfloat16)
                logit_grad = (
                    probs * (weight_grad - tile_rows[2:3]) * sharpness[:, lanes]
                ).astype(jnp.bfloat16)
                feature_grads[rows, lanes] = (
                    dot(weights, grad_rows[tile, group])
                    + dot(logit_grad, query_rows[tile, group])
                ).astype(jnp.bfloat16)
                part = gather_heads(dot_rows(weights, feature), n_cells)
                for sector in range(n_lon):
                    update[sector, :, lanes] += jnp.where(tile == sector, part, 0.0)
            return carry

        lax.fori_loop(first * n_blocks // 8, last * n_blocks // 8, four_blocks, 0)

    def out_grad(group):
        product = dot(hidden_t[...], feature_grads[:, lanes_of(group)])
        total[1 + group, :GROUP, :] = product[:, :PIECE]
        total[1 + group, GROUP:, :] = product[:, PIECE:]

    def perceptron_grad(index, carry):
        rows = rows_of(index, CHUNK)
        feature_grad = feature_grads[rows, :]
        hidden_grad = (dot(feature_grad, outer_t[...]) * slope[rows, :]).astype(jnp.bfloat16)
        product = dot(tokens_t[:, rows], hidden_grad)
        total[0, :GROUP, :] += product[:, :PIECE]
        total[0, GROUP:, :] += product[:, PIECE:]
        return carry

    sums_of = [sum_piece(piece, total, n_lat, n_lon, sum_refs) for piece in range(1 + groups)]

    def advance(*pieces):
        for piece in pieces:
            next(sums_of[piece])

    attend(0, 0, 2)
    out_grad(0)
    advance(1)
    attend(1, 0, 1)
    advance(1)
    attend(1, 1, 2)
    out_grad(1)
    advance(1, 2)
    attend(2, 0, 1)
    advance(1, 2)
    attend(2, 1, 2)
    update_out[...] = update[...].astype(jnp.bfloat16)
    arriving = [
        send(update_out.at[sectors[step]], update_in.at[step], up_send.at[step], up_recv.at[step],
             (lat, sectors[step], mem))
        for step in range(1, n_lon)]

    out_grad(2)
    advance(2, 3)
    chunks = n_tokens // CHUNK
    lax.fori_loop(0, chunks // 2, perceptron_grad, 0)
    advance(2, 3)
    lax.fori_loop(chunks // 2, chunks, perceptron_grad, 0)
    advance(0, 3)

    for copy in arriving:
        copy.wait()
    own_stats = tile_stats[lon]
    for group in range(groups):
        lanes = lanes_of(group)
        cells = latent[:, lanes].astype(jnp.float32)
        eye_shape = (GROUP, GROUP)
        eye = lax.broadcasted_iota(jnp.int32, eye_shape, 0) == lax.broadcasted_iota(
            jnp.int32, eye_shape, 1)
        self_weight = own_stats[3:4, lanes].astype(jnp.bfloat16).astype(jnp.float32)
        diagonal = jnp.where(eye, self_weight, 0.0).astype(jnp.bfloat16)
        own = dot(diagonal, spread_heads(cells).astype(jnp.bfloat16))
        change = update[lon, :, lanes] + gather_heads(own, n_cells)
        for step in range(1, n_lon):
            change = change + update_in[step, :, lanes].astype(jnp.float32)
        rounded = (cells + change).astype(jnp.bfloat16).astype(jnp.float32)
        state[:, :, lanes] = rounded.reshape(grid_rows, grid_cols, GROUP)
    for row in range(grid_rows):
        side[row : row + 1, :] = state[row, grid_cols - 1 : grid_cols, :]
        side[grid_rows + row : grid_rows + row + 1, :] = state[row, 0:1, :]
    rims_out[0] = state[0:2].reshape(16, width).astype(jnp.bfloat16)
    rims_out[1] = side[...].astype(jnp.bfloat16)
    rims_out[2] = state[grid_rows - 2 : grid_rows].reshape(16, width).astype(jnp.bfloat16)
    halos = []
    for index, (row_step, col_step) in enumerate(NEIGHBOURS):
        device = ((above, lat, below)[row_step + 1], lax.rem(lon + n_lon + col_step, n_lon), mem)
        halos.append(send(rims_out.at[row_step + 1], rims_in.at[index],
                          halo_send.at[index], halo_recv.at[index], device))

    advance(0, 3)
    for copy in halos:
        copy.wait()
    first, last = 8, 8 + grid_cols
    padded[1 : 1 + grid_rows, first:last, :] = state[...]
    for index, (row_step, col_step) in enumerate(NEIGHBOURS):
        rim = rims_in[index].astype(jnp.float32)
        if row_step == 0:
            place = first - 1 if col_step == 1 else last
            start = 0 if col_step == 1 else grid_rows
            for row in range(grid_rows):
                padded[1 + row, place : place + 1, :] = rim[start + row : start + row + 1]
        else:
            line = rim[16 - grid_cols :] * keep_above if row_step == 1 else rim[:grid_cols] * keep_below
            place = 0 if row_step == 1 else 1 + grid_rows
            if col_step == 0:
                padded[place, first:last, :] = line
            elif col_step == 1:
                padded[place, first - 1 : first, :] = line[grid_cols - 1 :]
            else:
                padded[place, last : last + 1, :] = line[:1]
    advance(0)
    for group in range(groups):
        lanes = lanes_of(group)
        mixed = padded[1 : 1 + grid_rows, first:last, lanes]
        for index, (row_step, col_step) in enumerate(NEIGHBOURS):
            mixed = mixed + mixing[index : index + 1, lanes] * padded[
                1 + row_step : 1 + row_step + grid_rows, first + col_step : last + col_step, lanes]
        analysis[:, lanes] = mixed.reshape(n_cells, GROUP).astype(jnp.bfloat16)
    advance(0)
    sums[...] = sum_refs[3][...].reshape(sums.shape)


def finish_kernel(analysis, sums, analysis_out, in_sum, out_sum):
    analysis_out[...] = analysis[...]
    in_sum[:, :PIECE] = sums[0, :GROUP].astype(jnp.float32)
    in_sum[:, PIECE:] = sums[0, GROUP:].astype(jnp.float32)
    for group in range(out_sum.shape[1] // GROUP):
        middle = group * GROUP + PIECE
        out_sum[:, middle - PIECE : middle] = sums[1 + group, :GROUP].astype(jnp.float32)
        out_sum[:, middle : middle + PIECE] = sums[1 + group, GROUP:].astype(jnp.float32)


def per_device(
    measured_inputs,
    target_sector,
    hidden_member_fields,
    analysis_adjoint,
    inner_perceptron_coeffs,
    outer_perceptron_coeffs,
    probe_projector,
    logit_sharpness,
    adjacent_channel_coeffs,
):
    n_lat, n_lon = lax.axis_size("lat"), lax.axis_size("lon")
    n_blocks, block_len, obs_width = measured_inputs.shape
    grid_rows, grid_cols, width = hidden_member_fields.shape[1:]
    hidden_width = inner_perceptron_coeffs.shape[1]
    n_cells = grid_rows * grid_cols
    n_tokens = n_blocks * block_len
    groups = width // GROUP
    roomy = n_lon <= 4
    bf16, f32 = jnp.bfloat16, jnp.float32
    vmem, dma = pltpu.VMEM, pltpu.SemaphoreType.DMA
    in_vmem = pl.BlockSpec(memory_space=pltpu.VMEM)
    spread = vmem((n_lon, groups, GROUP, GROUP), bf16)
    scratch = [
        vmem((n_lon, n_cells, width), bf16),
        vmem((n_lon, n_cells, width), bf16),
        vmem((n_lon, 16, width), bf16),
        vmem((n_lon, 16, width), bf16),
        vmem((grid_rows + 2, n_lon * grid_cols, width), f32),
        vmem((width, hidden_width), bf16),
        spread, spread, spread, spread,
        vmem((n_lon, 8, width), f32),
        vmem((n_tokens, width), bf16),
        vmem((n_tokens if roomy else 16, width), bf16),
        vmem((n_tokens if roomy else 8, width), f32),
        vmem((n_tokens if roomy else 8, width), f32),
        vmem((1, width), f32),
        vmem((hidden_width, n_tokens), bf16),
        vmem((obs_width, n_tokens), bf16),
        vmem((n_tokens, hidden_width), f32),
        vmem((n_blocks, 8, width), f32),
        vmem((n_lon, 4 * n_lon, width), f32),
        vmem((n_lon, 8, width), f32),
        vmem((n_lon, n_cells, width), f32),
        vmem((n_lon, n_cells, width), bf16),
        vmem((n_lon, n_cells, width), bf16),
        vmem((grid_rows, grid_cols, width), f32),
        vmem((16, width), f32),
        vmem((3, 16, width), bf16),
        vmem((8, 16, width), bf16),
        vmem((grid_rows + 2, 24, width), f32),
        vmem((1 + groups, 2 * GROUP, PIECE), f32),
        dma((n_lon,)), dma((n_lon,)), dma((n_lon,)), dma((n_lon,)),
        dma((2, n_lon)), dma((2, n_lon)),
        dma((n_lon,)), dma((n_lon,)), dma((n_lon,)), dma((n_lon,)),
        dma((8,)), dma((8,)),
    ] + sum_scratch(n_lat, n_lon, 1 + groups, 2 * GROUP)
    in_smem = pl.BlockSpec(memory_space=pltpu.SMEM)
    analysis, sums = pl.pallas_call(
        functools.partial(step_kernel, n_lat, n_lon, n_blocks, grid_rows, grid_cols, roomy),
        out_shape=[
            jax.ShapeDtypeStruct((n_cells, width), bf16),
            jax.ShapeDtypeStruct((1 + groups, 2 * GROUP, PIECE), bf16),
        ],
        in_specs=[in_smem] * 2 + [in_vmem] * 7,
        out_specs=[in_vmem] * 2,
        scratch_shapes=scratch,
        compiler_params=pltpu.CompilerParams(
            collective_id=0, has_side_effects=True, vmem_limit_bytes=60 << 20
        ),
        name="assimilation_step",
    )(
        target_sector,
        logit_sharpness,
        measured_inputs.reshape(n_tokens, obs_width),
        hidden_member_fields.reshape(n_cells, width),
        analysis_adjoint.reshape(n_cells, width),
        inner_perceptron_coeffs,
        outer_perceptron_coeffs,
        probe_projector,
        adjacent_channel_coeffs,
    )
    analysis, in_grad, out_grad = pl.pallas_call(
        finish_kernel,
        out_shape=[
            jax.ShapeDtypeStruct((n_cells, width), bf16),
            jax.ShapeDtypeStruct(inner_perceptron_coeffs.shape, f32),
            jax.ShapeDtypeStruct(outer_perceptron_coeffs.shape, f32),
        ],
        in_specs=[in_vmem] * 2,
        out_specs=[in_vmem] * 3,
        compiler_params=pltpu.CompilerParams(vmem_limit_bytes=16 << 20),
        name="to_float32",
    )(analysis, sums)
    return (analysis.reshape(hidden_member_fields.shape), in_grad, out_grad)


def solution(mesh):
    in_specs = (
        P(("lat", "lon", "mem"), None, None),
        P(("lat", "lon", "mem")),
        P("mem", "lat", "lon", None),
        P("mem", "lat", "lon", None),
        P(),
        P(),
        P(),
        P(),
        P(),
    )
    out_specs = (P("mem", "lat", "lon", None), P(), P())
    return jax.shard_map(
        per_device, mesh=mesh, in_specs=in_specs, out_specs=out_specs, check_vma=False
    )
```

```python
import functools
import math

import jax
import jax.numpy as jnp
from jax import lax
from jax.experimental import pallas as pl
from jax.experimental.pallas import tpu as pltpu
from jax.sharding import PartitionSpec as P

HEADS = 12
CHANNELS_PER_ATT = 64
GROUP = 256
CHUNK = 512
LOWEST = -1e30


NEIGHBOURS = ((-1, -1), (-1, 0), (-1, 1), (0, -1), (0, 1), (1, -1), (1, 0), (1, 1))

MESH = pl.DeviceIdType.MESH


def sum_scratch(n_lat, n_lon, rows, width):
    half = rows // 2
    part = half // n_lon
    return [
        pltpu.VMEM((rows, width), jnp.bfloat16),
        pltpu.VMEM((half, width), jnp.bfloat16),
        pltpu.VMEM((half, width), jnp.float32),
        pltpu.VMEM((n_lon, part, width), jnp.bfloat16),
        pltpu.VMEM((n_lon, part, width), jnp.bfloat16),
        pltpu.VMEM((n_lat, part, width), jnp.bfloat16),
        pltpu.VMEM((2, half, width), jnp.bfloat16),
        pltpu.SemaphoreType.DMA((2,)),
        pltpu.SemaphoreType.DMA((2,)),
        pltpu.SemaphoreType.DMA((2, n_lon)),
        pltpu.SemaphoreType.DMA((2, n_lon)),
        pltpu.SemaphoreType.DMA((n_lat,)),
        pltpu.SemaphoreType.DMA((n_lat,)),
    ]


def sum_stages(total, n_lat, n_lon, scratch):
    (rounded, from_core, half_sum, to_lon, from_lon, by_lat, whole,
     core_send, core_recv, lon_send, lon_recv, lat_send, lat_recv) = scratch
    lat, lon, mem = (lax.axis_index(name) for name in ("lat", "lon", "mem"))
    other = 1 - mem
    rows = total.shape[0]
    half = rows // 2
    part = half // n_lon

    rounded[...] = total[...].astype(jnp.bfloat16)
    away = pl.ds(pl.multiple_of(other * half, half), half)
    copy = pltpu.make_async_remote_copy(
        src_ref=rounded.at[away], dst_ref=from_core,
        send_sem=core_send.at[0], recv_sem=core_recv.at[0],
        device_id=(lat, lon, other), device_id_type=MESH)
    copy.start()
    yield
    copy.wait()
    mine = pl.ds(pl.multiple_of(mem * half, half), half)
    half_sum[...] = total[mine, :] + from_core[...].astype(jnp.float32)

    to_lon[...] = half_sum[...].astype(jnp.bfloat16).reshape(to_lon.shape)
    copies = []
    for step in range(1, n_lon):
        peer = lax.rem(lon + step, n_lon)
        copy = pltpu.make_async_remote_copy(
            src_ref=to_lon.at[peer], dst_ref=from_lon.at[step],
            send_sem=lon_send.at[0, step], recv_sem=lon_recv.at[0, step],
            device_id=(lat, peer, mem), device_id_type=MESH)
        copy.start()
        copies.append(copy)
    yield
    part_sum = half_sum[pl.ds(pl.multiple_of(lon * part, part), part), :]
    for step, copy in enumerate(copies, 1):
        copy.wait()
        part_sum = part_sum + from_lon[step].astype(jnp.float32)

    by_lat[lat] = part_sum.astype(jnp.bfloat16)
    copies = []
    for step in range(1, n_lat):
        peer = lax.rem(lat + step, n_lat)
        copy = pltpu.make_async_remote_copy(
            src_ref=by_lat.at[lat], dst_ref=by_lat.at[lat],
            send_sem=lat_send.at[step], recv_sem=lat_recv.at[step],
            device_id=(peer, lon, mem), device_id_type=MESH)
        copy.start()
        copies.append(copy)
    yield
    for copy in copies:
        copy.wait()
    band_sum = by_lat[0].astype(jnp.float32)
    for index in range(1, n_lat):
        band_sum = band_sum + by_lat[index].astype(jnp.float32)

    own = pl.ds(pl.multiple_of(lon * part, part), part)
    whole[mem, own, :] = band_sum.astype(jnp.bfloat16)
    copies = []
    for step in range(1, n_lon):
        peer = lax.rem(lon + step, n_lon)
        copy = pltpu.make_async_remote_copy(
            src_ref=whole.at[mem, own], dst_ref=whole.at[mem, own],
            send_sem=lon_send.at[1, step], recv_sem=lon_recv.at[1, step],
            device_id=(lat, peer, mem), device_id_type=MESH)
        copy.start()
        copies.append(copy)
    yield
    for copy in copies:
        copy.wait()
    copy = pltpu.make_async_remote_copy(
        src_ref=whole.at[mem], dst_ref=whole.at[mem],
        send_sem=core_send.at[1], recv_sem=core_recv.at[1],
        device_id=(lat, lon, other), device_id_type=MESH)
    copy.start()
    yield
    copy.wait()
    yield


def greet(partners):
    barrier = pltpu.get_barrier_semaphore()
    for partner in partners:
        pl.semaphore_signal(barrier, inc=1, device_id=partner, device_id_type=MESH)
    pl.semaphore_wait(barrier, len(partners))


def rows_of(index, size):
    return pl.ds(pl.multiple_of(index * size, size), size)


def lanes_of(group):
    return slice(group * GROUP, (group + 1) * GROUP)


def dot(left, right):
    return jnp.dot(left, right, preferred_element_type=jnp.float32)


def dot_rows(left, right):
    return lax.dot_general(
        left, right, (((0,), (0,)), ((), ())), preferred_element_type=jnp.float32
    )


def spread_heads(cells):
    tall = jnp.concatenate([cells] * (GROUP // CHANNELS_PER_ATT), axis=0)
    row_head = lax.broadcasted_iota(jnp.int32, tall.shape, 0) // cells.shape[0]
    col_head = lax.broadcasted_iota(jnp.int32, tall.shape, 1) // CHANNELS_PER_ATT
    return jnp.where(row_head == col_head, tall, 0.0)


def spread_heads_t(cells):
    n_cells = cells.shape[0]
    twice = jnp.concatenate([cells, cells], axis=0).T
    wide = jnp.concatenate([twice] * (GROUP // CHANNELS_PER_ATT // 2), axis=1)
    row_head = lax.broadcasted_iota(jnp.int32, wide.shape, 0) // CHANNELS_PER_ATT
    col_head = lax.broadcasted_iota(jnp.int32, wide.shape, 1) // n_cells
    return jnp.where(row_head == col_head, wide, 0.0)


def gather_heads(tall, n_cells):
    col_head = lax.broadcasted_iota(jnp.int32, (n_cells, GROUP), 1) // CHANNELS_PER_ATT
    cells = tall[:n_cells]
    for head in range(1, GROUP // CHANNELS_PER_ATT):
        cells = jnp.where(col_head == head, tall[head * n_cells : (head + 1) * n_cells], cells)
    return cells


def step_kernel(
    n_lat, n_lon, n_blocks, grid_rows, grid_cols, roomy,
    targets, head_sharpness, tokens, latent, cotangent, inner, outer, projector, mixing,
    analysis, sums,
    latents, cots, cots_above, cots_below, band, outer_t,
    query_rows, query_cols, grad_rows, grad_cols, self_rows,
    features, kept, kept_scores, kept_grads, sharpness, hidden, slope, block_stats, stats, tile_stats,
    update, update_out, update_in, state, side, rims_out, rims_in, padded, total,
    lat_send, lat_recv, cot_send, cot_recv, rim_send, rim_recv,
    stat_send, stat_recv, up_send, up_recv, halo_send, halo_recv,
    *sum_refs,
):
    lat, lon, mem = (lax.axis_index(name) for name in ("lat", "lon", "mem"))
    n_cells, width = latent.shape
    feature_grads = kept if roomy else features
    grads = update
    n_tokens = tokens.shape[0]
    block_len = n_tokens // n_blocks
    groups = width // GROUP
    above, below = lax.rem(lat + n_lat - 1, n_lat), lax.rem(lat + 1, n_lat)
    keep_above = jnp.where(lat > 0, 1.0, 0.0)
    keep_below = jnp.where(lat < n_lat - 1, 1.0, 0.0)
    sectors = [lax.rem(lon + step, n_lon) for step in range(n_lon)]

    partners = [(lat, lon, 1 - mem)]
    partners += [(lat, sector, mem) for sector in sectors[1:]]
    partners += [(row, sector, mem) for row in (above, below) for sector in sectors]
    partners += [(lax.rem(lat + step, n_lat), lon, mem) for step in range(2, n_lat - 1)]
    greet(partners)

    def send(src, dst, send_sem, recv_sem, device):
        copy = pltpu.make_async_remote_copy(
            src_ref=src, dst_ref=dst, send_sem=send_sem, recv_sem=recv_sem,
            device_id=device, device_id_type=MESH)
        copy.start()
        return copy

    arriving = []
    for step in range(1, n_lon):
        arriving.append(send(latent, latents.at[lon], lat_send.at[step], lat_recv.at[step],
                             (lat, sectors[step], mem)))
    for step in range(1, n_lon):
        arriving.append(send(cotangent, cots.at[lon], cot_send.at[step], cot_recv.at[step],
                             (lat, sectors[step], mem)))
    for step in range(n_lon):
        arriving.append(send(cotangent.at[pl.ds(n_cells - 16, 16)], cots_above.at[lon],
                             rim_send.at[0, step], rim_recv.at[0, step],
                             (below, sectors[step], mem)))
        arriving.append(send(cotangent.at[pl.ds(0, 16)], cots_below.at[lon],
                             rim_send.at[1, step], rim_recv.at[1, step],
                             (above, sectors[step], mem)))
    head = lax.broadcasted_iota(jnp.int32, (1, width), 1) // CHANNELS_PER_ATT
    row = jnp.zeros((1, width), jnp.float32)
    for index in range(HEADS):
        row = jnp.where(head == index, head_sharpness[index], row)
    sharpness[...] = row / math.sqrt(CHANNELS_PER_ATT)
    latents[lon] = latent[...]
    cots[lon] = cotangent[...]
    outer_t[...] = outer[...].astype(jnp.float32).T.astype(jnp.bfloat16)

    def perceptron(index, carry):
        rows = rows_of(index, CHUNK)
        pre_act = dot(tokens[rows, :], inner[...])
        sigmoid_val = jax.nn.sigmoid(pre_act)
        slope[rows, :] = sigmoid_val * (1.0 + pre_act * (1.0 - sigmoid_val))
        hidden_act = (pre_act * sigmoid_val).astype(jnp.bfloat16)
        hidden[rows, :] = hidden_act
        features[rows, :] = dot(hidden_act, outer[...]).astype(jnp.bfloat16)
        return carry

    lax.fori_loop(0, n_tokens // CHUNK, perceptron, 0)
    for copy in arriving[: n_lon - 1]:
        copy.wait()

    def prepare_queries(tile, carry):
        query = dot(latents[tile], projector[...]).astype(jnp.bfloat16).astype(jnp.float32)
        for group in range(groups):
            lanes = lanes_of(group)
            cell_t = spread_heads_t(latents[tile, :, lanes].astype(jnp.float32))
            spread_t = spread_heads_t(query[:, lanes])
            query_rows[tile, group] = spread_heads(query[:, lanes]).astype(jnp.bfloat16)
            query_cols[tile, group] = spread_t.astype(jnp.bfloat16)
            self_rows[tile, 0:1, lanes] = (
                jnp.sum(spread_t * cell_t, axis=0, keepdims=True) * sharpness[:, lanes])
        return carry

    lax.fori_loop(0, n_lon, prepare_queries, 0)
    for copy in arriving[n_lon - 1 :]:
        copy.wait()

    for tile in range(n_lon):
        cols = slice(tile * grid_cols, (tile + 1) * grid_cols)
        band[1 : 1 + grid_rows, cols, :] = (
            cots[tile].astype(jnp.float32).reshape(grid_rows, grid_cols, width))
        band[0, cols, :] = cots_above[tile].astype(jnp.float32)[16 - grid_cols :] * keep_above
        band[1 + grid_rows, cols, :] = cots_below[tile].astype(jnp.float32)[:grid_cols] * keep_below

    def mix_row(row, carry):
        for group in range(groups):
            lanes = lanes_of(group)
            mixed = band[1 + row, :, lanes]
            for index, (row_step, col_step) in enumerate(NEIGHBOURS):
                line = band[1 + row - row_step, :, lanes]
                if col_step:
                    line = pltpu.roll(line, col_step % (n_lon * grid_cols), 0)
                mixed = mixed + mixing[index : index + 1, lanes] * line
            mixed = mixed.astype(jnp.bfloat16).astype(jnp.float32)
            for tile in range(n_lon):
                grads[tile, rows_of(row, grid_cols), lanes] = (
                    mixed[tile * grid_cols : (tile + 1) * grid_cols])
        return carry

    lax.fori_loop(0, grid_rows, mix_row, 0)

    def prepare_grads(tile, carry):
        for group in range(groups):
            lanes = lanes_of(group)
            cell_t = spread_heads_t(latents[tile, :, lanes].astype(jnp.float32))
            spread_t = spread_heads_t(grads[tile, :, lanes])
            grad_rows[tile, group] = spread_heads(grads[tile, :, lanes]).astype(jnp.bfloat16)
            grad_cols[tile, group] = spread_t.astype(jnp.bfloat16)
            self_rows[tile, 1:2, lanes] = jnp.sum(spread_t * cell_t, axis=0, keepdims=True)
        return carry

    lax.fori_loop(0, n_lon, prepare_grads, 0)

    def block_sums(pair, carry):
        for block, group in [(2 * pair + i, j) for i in range(2) for j in range(groups)]:
            tile = targets[block]
            rows = rows_of(block, block_len)
            lanes = lanes_of(group)
            feature = features[rows, lanes]
            scores = dot(feature, query_cols[tile, group]) * sharpness[:, lanes]
            weight_grad = dot(feature, grad_cols[tile, group])
            if roomy:
                kept_scores[rows, lanes] = scores
                kept_grads[rows, lanes] = weight_grad
            top = jnp.max(scores, axis=0, keepdims=True)
            exp_terms = jnp.exp(scores - top)
            block_stats[block, 0:1, lanes] = top
            block_stats[block, 1:2, lanes] = jnp.sum(exp_terms, axis=0, keepdims=True)
            block_stats[block, 2:3, lanes] = jnp.sum(
                exp_terms * weight_grad, axis=0, keepdims=True)
        return carry

    lax.fori_loop(0, n_blocks // 2, block_sums, 0)

    for tile in range(n_lon):
        tops = [jnp.where(targets[block] == tile, block_stats[block, 0:1, :], LOWEST)
                for block in range(n_blocks)]
        top = functools.reduce(jnp.maximum, tops)
        exp_sum = jnp.zeros_like(top)
        grad_sum = jnp.zeros_like(top)
        for block in range(n_blocks):
            scale = jnp.exp(tops[block] - top)
            scale = jnp.where(targets[block] == tile, scale, 0.0)
            exp_sum = exp_sum + scale * block_stats[block, 1:2, :]
            grad_sum = grad_sum + scale * block_stats[block, 2:3, :]
        stats[lon, 4 * tile : 4 * tile + 1, :] = top
        stats[lon, 4 * tile + 1 : 4 * tile + 2, :] = exp_sum
        stats[lon, 4 * tile + 2 : 4 * tile + 3, :] = grad_sum
        stats[lon, 4 * tile + 3 : 4 * tile + 4, :] = jnp.zeros_like(top)

    arriving = [
        send(stats.at[lon], stats.at[lon], stat_send.at[step], stat_recv.at[step],
             (lat, sectors[step], mem))
        for step in range(1, n_lon)]
    update[...] = jnp.zeros_like(update)
    total[...] = jnp.zeros_like(total)
    for copy in arriving:
        copy.wait()

    for tile in range(n_lon):
        self_score = self_rows[tile, 0:1, :]
        top = self_score
        for sector in range(n_lon):
            top = jnp.maximum(top, stats[sector, 4 * tile : 4 * tile + 1, :])
        self_exp = jnp.exp(self_score - top)
        exp_sum = self_exp
        grad_sum = self_exp * self_rows[tile, 1:2, :]
        for sector in range(n_lon):
            scale = jnp.exp(stats[sector, 4 * tile : 4 * tile + 1, :] - top)
            exp_sum = exp_sum + scale * stats[sector, 4 * tile + 1 : 4 * tile + 2, :]
            grad_sum = grad_sum + scale * stats[sector, 4 * tile + 2 : 4 * tile + 3, :]
        inverse = 1.0 / exp_sum
        tile_stats[tile, 0:1, :] = top
        tile_stats[tile, 1:2, :] = inverse
        tile_stats[tile, 2:3, :] = grad_sum * inverse
        tile_stats[tile, 3:4, :] = self_exp * inverse

    def attend(chosen, count, step, carry):
        for block, group in [(count * step + i, j) for i in range(count) for j in chosen]:
            tile = targets[block]
            rows = rows_of(block, block_len)
            lanes = lanes_of(group)
            feature = features[rows, lanes]
            if roomy:
                scores = kept_scores[rows, lanes]
                weight_grad = kept_grads[rows, lanes]
            else:
                scores = dot(feature, query_cols[tile, group]) * sharpness[:, lanes]
                weight_grad = dot(feature, grad_cols[tile, group])
            tile_rows = tile_stats[tile, :, lanes]
            probs = jnp.exp(scores - tile_rows[0:1]) * tile_rows[1:2]
            weights = probs.astype(jnp.bfloat16)
            logit_grad = (
                probs * (weight_grad - tile_rows[2:3]) * sharpness[:, lanes]
            ).astype(jnp.bfloat16)
            feature_grads[rows, lanes] = (
                dot(weights, grad_rows[tile, group]) + dot(logit_grad, query_rows[tile, group])
            ).astype(jnp.bfloat16)
            part = gather_heads(dot_rows(weights, feature), n_cells)
            for sector in range(n_lon):
                update[sector, :, lanes] += jnp.where(tile == sector, part, 0.0)
        return carry

    def attend_loop(chosen, first, last):
        count = 4 // len(chosen)
        body = functools.partial(attend, chosen, count)
        lax.fori_loop(first * n_blocks // (8 * count), last * n_blocks // (8 * count), body, 0)

    def out_grad(index, carry):
        rows = rows_of(index, CHUNK)
        product = dot_rows(hidden[rows, :], feature_grads[rows, : 2 * GROUP])
        total[0, :GROUP, :] += product[:, :GROUP]
        total[0, GROUP:, :] += product[:, GROUP:]
        return carry

    first_sum, last_sum = [
        sum_stages(total.at[index], n_lat, n_lon, sum_refs[index :: 2]) for index in range(2)]
    chunks = n_tokens // CHUNK
    attend_loop((0, 1), 0, 8)
    lax.fori_loop(0, chunks, out_grad, 0)
    next(first_sum)
    attend_loop((2,), 0, 4)
    next(first_sum)
    attend_loop((2,), 4, 8)
    next(first_sum)
    update_out[...] = update[...].astype(jnp.bfloat16)
    arriving = [
        send(update_out.at[sectors[step]], update_in.at[step], up_send.at[step], up_recv.at[step],
             (lat, sectors[step], mem))
        for step in range(1, n_lon)]

    def perceptron_grad(index, carry):
        rows = rows_of(index, CHUNK)
        feature_grad = feature_grads[rows, :]
        hidden_grad = (dot(feature_grad, outer_t[...]) * slope[rows, :]).astype(jnp.bfloat16)
        total[1, :GROUP, :] += dot_rows(tokens[rows, :], hidden_grad)
        total[1, GROUP:, :] += dot_rows(hidden[rows, :], feature_grad[:, 2 * GROUP :])
        return carry

    lax.fori_loop(0, chunks // 2, perceptron_grad, 0)
    next(first_sum)
    lax.fori_loop(chunks // 2, chunks, perceptron_grad, 0)
    next(last_sum)
    next(first_sum)

    for copy in arriving:
        copy.wait()
    own_stats = tile_stats[lon]
    for group in range(groups):
        lanes = lanes_of(group)
        cells = latent[:, lanes].astype(jnp.float32)
        eye_shape = (GROUP, GROUP)
        eye = lax.broadcasted_iota(jnp.int32, eye_shape, 0) == lax.broadcasted_iota(
            jnp.int32, eye_shape, 1)
        self_weight = own_stats[3:4, lanes].astype(jnp.bfloat16).astype(jnp.float32)
        diagonal = jnp.where(eye, self_weight, 0.0).astype(jnp.bfloat16)
        own = dot(diagonal, spread_heads(cells).astype(jnp.bfloat16))
        change = update[lon, :, lanes] + gather_heads(own, n_cells)
        for step in range(1, n_lon):
            change = change + update_in[step, :, lanes].astype(jnp.float32)
        rounded = (cells + change).astype(jnp.bfloat16).astype(jnp.float32)
        state[:, :, lanes] = rounded.reshape(grid_rows, grid_cols, GROUP)
    for row in range(grid_rows):
        side[row : row + 1, :] = state[row, grid_cols - 1 : grid_cols, :]
        side[grid_rows + row : grid_rows + row + 1, :] = state[row, 0:1, :]
    rims_out[0] = state[0:2].reshape(16, width).astype(jnp.bfloat16)
    rims_out[1] = side[...].astype(jnp.bfloat16)
    rims_out[2] = state[grid_rows - 2 : grid_rows].reshape(16, width).astype(jnp.bfloat16)
    halos = []
    for index, (row_step, col_step) in enumerate(NEIGHBOURS):
        device = ((above, lat, below)[row_step + 1], lax.rem(lon + n_lon + col_step, n_lon), mem)
        halos.append(send(rims_out.at[row_step + 1], rims_in.at[index],
                          halo_send.at[index], halo_recv.at[index], device))

    next(last_sum)
    next(first_sum)
    next(last_sum)
    for copy in halos:
        copy.wait()
    first, last = 8, 8 + grid_cols
    padded[1 : 1 + grid_rows, first:last, :] = state[...]
    for index, (row_step, col_step) in enumerate(NEIGHBOURS):
        rim = rims_in[index].astype(jnp.float32)
        if row_step == 0:
            place = first - 1 if col_step == 1 else last
            start = 0 if col_step == 1 else grid_rows
            for row in range(grid_rows):
                padded[1 + row, place : place + 1, :] = rim[start + row : start + row + 1]
        else:
            line = rim[16 - grid_cols :] * keep_above if row_step == 1 else rim[:grid_cols] * keep_below
            place = 0 if row_step == 1 else 1 + grid_rows
            if col_step == 0:
                padded[place, first:last, :] = line
            elif col_step == 1:
                padded[place, first - 1 : first, :] = line[grid_cols - 1 :]
            else:
                padded[place, last : last + 1, :] = line[:1]
    next(last_sum)
    for group in range(groups):
        lanes = lanes_of(group)
        mixed = padded[1 : 1 + grid_rows, first:last, lanes]
        for index, (row_step, col_step) in enumerate(NEIGHBOURS):
            mixed = mixed + mixing[index : index + 1, lanes] * padded[
                1 + row_step : 1 + row_step + grid_rows, first + col_step : last + col_step, lanes]
        analysis[:, lanes] = mixed.reshape(n_cells, GROUP).astype(jnp.bfloat16)
    next(last_sum)
    next(last_sum)
    sums[0] = sum_refs[12][...]
    sums[1] = sum_refs[13][...]


def finish_kernel(analysis, sums, analysis_out, in_sum, out_sum):
    analysis_out[...] = analysis[...]
    in_sum[...] = sums[1, 0].astype(jnp.float32)
    for group, (index, part) in enumerate(((0, 0), (0, 1), (1, 1))):
        out_sum[:, lanes_of(group)] = sums[index, part].astype(jnp.float32)


def per_device(
    measured_inputs,
    target_sector,
    hidden_member_fields,
    analysis_adjoint,
    inner_perceptron_coeffs,
    outer_perceptron_coeffs,
    probe_projector,
    logit_sharpness,
    adjacent_channel_coeffs,
):
    n_lat, n_lon = lax.axis_size("lat"), lax.axis_size("lon")
    n_blocks, block_len, obs_width = measured_inputs.shape
    grid_rows, grid_cols, width = hidden_member_fields.shape[1:]
    hidden_width = inner_perceptron_coeffs.shape[1]
    n_cells = grid_rows * grid_cols
    n_tokens = n_blocks * block_len
    groups = width // GROUP
    roomy = n_lon <= 4
    bf16, f32 = jnp.bfloat16, jnp.float32
    vmem, dma = pltpu.VMEM, pltpu.SemaphoreType.DMA
    in_vmem = pl.BlockSpec(memory_space=pltpu.VMEM)
    spread = vmem((n_lon, groups, GROUP, GROUP), bf16)
    scratch = [
        vmem((n_lon, n_cells, width), bf16),
        vmem((n_lon, n_cells, width), bf16),
        vmem((n_lon, 16, width), bf16),
        vmem((n_lon, 16, width), bf16),
        vmem((grid_rows + 2, n_lon * grid_cols, width), f32),
        vmem((width, hidden_width), bf16),
        spread, spread, spread, spread,
        vmem((n_lon, 8, width), f32),
        vmem((n_tokens, width), bf16),
        vmem((n_tokens if roomy else 16, width), bf16),
        vmem((n_tokens if roomy else 8, width), f32),
        vmem((n_tokens if roomy else 8, width), f32),
        vmem((1, width), f32),
        vmem((n_tokens, hidden_width), bf16),
        vmem((n_tokens, hidden_width), f32),
        vmem((n_blocks, 8, width), f32),
        vmem((n_lon, 4 * n_lon, width), f32),
        vmem((n_lon, 8, width), f32),
        vmem((n_lon, n_cells, width), f32),
        vmem((n_lon, n_cells, width), bf16),
        vmem((n_lon, n_cells, width), bf16),
        vmem((grid_rows, grid_cols, width), f32),
        vmem((16, width), f32),
        vmem((3, 16, width), bf16),
        vmem((8, 16, width), bf16),
        vmem((grid_rows + 2, 24, width), f32),
        vmem((2, 2 * GROUP, GROUP), f32),
        dma((n_lon,)), dma((n_lon,)), dma((n_lon,)), dma((n_lon,)),
        dma((2, n_lon)), dma((2, n_lon)),
        dma((n_lon,)), dma((n_lon,)), dma((n_lon,)), dma((n_lon,)),
        dma((8,)), dma((8,)),
    ] + [
        ref for ref in sum_scratch(n_lat, n_lon, 2 * GROUP, GROUP) for _ in range(2)
    ]
    in_smem = pl.BlockSpec(memory_space=pltpu.SMEM)
    analysis, sums = pl.pallas_call(
        functools.partial(step_kernel, n_lat, n_lon, n_blocks, grid_rows, grid_cols, roomy),
        out_shape=[
            jax.ShapeDtypeStruct((n_cells, width), bf16),
            jax.ShapeDtypeStruct((2, 2, GROUP, GROUP), bf16),
        ],
        in_specs=[in_smem] * 2 + [in_vmem] * 7,
        out_specs=[in_vmem] * 2,
        scratch_shapes=scratch,
        compiler_params=pltpu.CompilerParams(
            collective_id=0, has_side_effects=True, vmem_limit_bytes=60 << 20
        ),
        name="assimilation_step",
    )(
        target_sector,
        logit_sharpness,
        measured_inputs.reshape(n_tokens, obs_width),
        hidden_member_fields.reshape(n_cells, width),
        analysis_adjoint.reshape(n_cells, width),
        inner_perceptron_coeffs,
        outer_perceptron_coeffs,
        probe_projector,
        adjacent_channel_coeffs,
    )
    analysis, in_grad, out_grad = pl.pallas_call(
        finish_kernel,
        out_shape=[
            jax.ShapeDtypeStruct((n_cells, width), bf16),
            jax.ShapeDtypeStruct(inner_perceptron_coeffs.shape, f32),
            jax.ShapeDtypeStruct(outer_perceptron_coeffs.shape, f32),
        ],
        in_specs=[in_vmem] * 2,
        out_specs=[in_vmem] * 3,
        compiler_params=pltpu.CompilerParams(vmem_limit_bytes=16 << 20),
        name="to_float32",
    )(analysis, sums)
    return (analysis.reshape(hidden_member_fields.shape), in_grad, out_grad)


def solution(mesh):
    in_specs = (
        P(("lat", "lon", "mem"), None, None),
        P(("lat", "lon", "mem")),
        P("mem", "lat", "lon", None),
        P("mem", "lat", "lon", None),
        P(),
        P(),
        P(),
        P(),
        P(),
    )
    out_specs = (P("mem", "lat", "lon", None), P(), P())
    return jax.shard_map(
        per_device, mesh=mesh, in_specs=in_specs, out_specs=out_specs, check_vma=False
    )
```

```python
import functools
import math

import jax
import jax.numpy as jnp
from jax import lax
from jax.experimental import pallas as pl
from jax.experimental.pallas import tpu as pltpu
from jax.sharding import PartitionSpec as P

HEADS = 12
CHANNELS_PER_ATT = 64
GROUP = 256
CHUNK = 512
LOWEST = -1e30


NEIGHBOURS = ((-1, -1), (-1, 0), (-1, 1), (0, -1), (0, 1), (1, -1), (1, 0), (1, 1))

MESH = pl.DeviceIdType.MESH


def sum_scratch(n_lat, n_lon, rows, width):
    half = rows // 2
    part = half // n_lon
    return [
        pltpu.VMEM((rows, width), jnp.bfloat16),
        pltpu.VMEM((half, width), jnp.bfloat16),
        pltpu.VMEM((half, width), jnp.float32),
        pltpu.VMEM((n_lon, part, width), jnp.bfloat16),
        pltpu.VMEM((n_lon, part, width), jnp.bfloat16),
        pltpu.VMEM((n_lat, part, width), jnp.bfloat16),
        pltpu.VMEM((2, half, width), jnp.bfloat16),
        pltpu.SemaphoreType.DMA((2,)),
        pltpu.SemaphoreType.DMA((2,)),
        pltpu.SemaphoreType.DMA((2, n_lon)),
        pltpu.SemaphoreType.DMA((2, n_lon)),
        pltpu.SemaphoreType.DMA((n_lat,)),
        pltpu.SemaphoreType.DMA((n_lat,)),
    ]


def sum_over_devices(total, n_lat, n_lon, scratch):
    (rounded, from_core, half_sum, to_lon, from_lon, by_lat, whole,
     core_send, core_recv, lon_send, lon_recv, lat_send, lat_recv) = scratch
    lat, lon, mem = (lax.axis_index(name) for name in ("lat", "lon", "mem"))
    other = 1 - mem
    rows = total.shape[0]
    half = rows // 2
    part = half // n_lon

    rounded[...] = total[...].astype(jnp.bfloat16)
    away = pl.ds(pl.multiple_of(other * half, half), half)
    copy = pltpu.make_async_remote_copy(
        src_ref=rounded.at[away], dst_ref=from_core,
        send_sem=core_send.at[0], recv_sem=core_recv.at[0],
        device_id=(lat, lon, other), device_id_type=MESH)
    copy.start()
    copy.wait()
    mine = pl.ds(pl.multiple_of(mem * half, half), half)
    half_sum[...] = total[mine, :] + from_core[...].astype(jnp.float32)

    to_lon[...] = half_sum[...].astype(jnp.bfloat16).reshape(to_lon.shape)
    copies = []
    for step in range(1, n_lon):
        peer = lax.rem(lon + step, n_lon)
        copy = pltpu.make_async_remote_copy(
            src_ref=to_lon.at[peer], dst_ref=from_lon.at[step],
            send_sem=lon_send.at[0, step], recv_sem=lon_recv.at[0, step],
            device_id=(lat, peer, mem), device_id_type=MESH)
        copy.start()
        copies.append(copy)
    part_sum = half_sum[pl.ds(pl.multiple_of(lon * part, part), part), :]
    for step, copy in enumerate(copies, 1):
        copy.wait()
        part_sum = part_sum + from_lon[step].astype(jnp.float32)

    by_lat[lat] = part_sum.astype(jnp.bfloat16)
    copies = []
    for step in range(1, n_lat):
        peer = lax.rem(lat + step, n_lat)
        copy = pltpu.make_async_remote_copy(
            src_ref=by_lat.at[lat], dst_ref=by_lat.at[lat],
            send_sem=lat_send.at[step], recv_sem=lat_recv.at[step],
            device_id=(peer, lon, mem), device_id_type=MESH)
        copy.start()
        copies.append(copy)
    for copy in copies:
        copy.wait()
    band_sum = by_lat[0].astype(jnp.float32)
    for index in range(1, n_lat):
        band_sum = band_sum + by_lat[index].astype(jnp.float32)

    own = pl.ds(pl.multiple_of(lon * part, part), part)
    whole[mem, own, :] = band_sum.astype(jnp.bfloat16)
    copies = []
    for step in range(1, n_lon):
        peer = lax.rem(lon + step, n_lon)
        copy = pltpu.make_async_remote_copy(
            src_ref=whole.at[mem, own], dst_ref=whole.at[mem, own],
            send_sem=lon_send.at[1, step], recv_sem=lon_recv.at[1, step],
            device_id=(lat, peer, mem), device_id_type=MESH)
        copy.start()
        copies.append(copy)
    for copy in copies:
        copy.wait()
    copy = pltpu.make_async_remote_copy(
        src_ref=whole.at[mem], dst_ref=whole.at[mem],
        send_sem=core_send.at[1], recv_sem=core_recv.at[1],
        device_id=(lat, lon, other), device_id_type=MESH)
    copy.start()
    copy.wait()
    return whole


def greet(partners):
    barrier = pltpu.get_barrier_semaphore()
    for partner in partners:
        pl.semaphore_signal(barrier, inc=1, device_id=partner, device_id_type=MESH)
    pl.semaphore_wait(barrier, len(partners))


def rows_of(index, size):
    return pl.ds(pl.multiple_of(index * size, size), size)


def lanes_of(group):
    return slice(group * GROUP, (group + 1) * GROUP)


def dot(left, right):
    return jnp.dot(left, right, preferred_element_type=jnp.float32)


def dot_rows(left, right):
    return lax.dot_general(
        left, right, (((0,), (0,)), ((), ())), preferred_element_type=jnp.float32
    )


def spread_heads(cells):
    tall = jnp.concatenate([cells] * (GROUP // CHANNELS_PER_ATT), axis=0)
    row_head = lax.broadcasted_iota(jnp.int32, tall.shape, 0) // cells.shape[0]
    col_head = lax.broadcasted_iota(jnp.int32, tall.shape, 1) // CHANNELS_PER_ATT
    return jnp.where(row_head == col_head, tall, 0.0)


def spread_heads_t(cells):
    n_cells = cells.shape[0]
    twice = jnp.concatenate([cells, cells], axis=0).T
    wide = jnp.concatenate([twice] * (GROUP // CHANNELS_PER_ATT // 2), axis=1)
    row_head = lax.broadcasted_iota(jnp.int32, wide.shape, 0) // CHANNELS_PER_ATT
    col_head = lax.broadcasted_iota(jnp.int32, wide.shape, 1) // n_cells
    return jnp.where(row_head == col_head, wide, 0.0)


def gather_heads(tall, n_cells):
    col_head = lax.broadcasted_iota(jnp.int32, (n_cells, GROUP), 1) // CHANNELS_PER_ATT
    cells = tall[:n_cells]
    for head in range(1, GROUP // CHANNELS_PER_ATT):
        cells = jnp.where(col_head == head, tall[head * n_cells : (head + 1) * n_cells], cells)
    return cells


def step_kernel(
    n_lat, n_lon, n_blocks, grid_rows, grid_cols, roomy,
    targets, head_sharpness, tokens, latent, cotangent, inner, outer, projector, mixing,
    analysis, sums,
    latents, cots, cots_above, cots_below, band, outer_t,
    query_rows, query_cols, grad_rows, grad_cols, self_rows,
    features, kept, kept_scores, kept_grads, sharpness, hidden, slope, block_stats, stats, tile_stats,
    update, update_out, update_in, state, side, rims_out, rims_in, padded, total,
    lat_send, lat_recv, cot_send, cot_recv, rim_send, rim_recv,
    stat_send, stat_recv, up_send, up_recv, halo_send, halo_recv,
    *sum_refs,
):
    lat, lon, mem = (lax.axis_index(name) for name in ("lat", "lon", "mem"))
    n_cells, width = latent.shape
    feature_grads = kept if roomy else features
    grads = update
    n_tokens = tokens.shape[0]
    block_len = n_tokens // n_blocks
    groups = width // GROUP
    above, below = lax.rem(lat + n_lat - 1, n_lat), lax.rem(lat + 1, n_lat)
    keep_above = jnp.where(lat > 0, 1.0, 0.0)
    keep_below = jnp.where(lat < n_lat - 1, 1.0, 0.0)
    sectors = [lax.rem(lon + step, n_lon) for step in range(n_lon)]

    partners = [(lat, lon, 1 - mem)]
    partners += [(lat, sector, mem) for sector in sectors[1:]]
    partners += [(row, sector, mem) for row in (above, below) for sector in sectors]
    partners += [(lax.rem(lat + step, n_lat), lon, mem) for step in range(2, n_lat - 1)]
    greet(partners)

    def send(src, dst, send_sem, recv_sem, device):
        copy = pltpu.make_async_remote_copy(
            src_ref=src, dst_ref=dst, send_sem=send_sem, recv_sem=recv_sem,
            device_id=device, device_id_type=MESH)
        copy.start()
        return copy

    arriving = []
    for step in range(1, n_lon):
        arriving.append(send(latent, latents.at[lon], lat_send.at[step], lat_recv.at[step],
                             (lat, sectors[step], mem)))
    for step in range(1, n_lon):
        arriving.append(send(cotangent, cots.at[lon], cot_send.at[step], cot_recv.at[step],
                             (lat, sectors[step], mem)))
    for step in range(n_lon):
        arriving.append(send(cotangent.at[pl.ds(n_cells - 16, 16)], cots_above.at[lon],
                             rim_send.at[0, step], rim_recv.at[0, step],
                             (below, sectors[step], mem)))
        arriving.append(send(cotangent.at[pl.ds(0, 16)], cots_below.at[lon],
                             rim_send.at[1, step], rim_recv.at[1, step],
                             (above, sectors[step], mem)))
    head = lax.broadcasted_iota(jnp.int32, (1, width), 1) // CHANNELS_PER_ATT
    row = jnp.zeros((1, width), jnp.float32)
    for index in range(HEADS):
        row = jnp.where(head == index, head_sharpness[index], row)
    sharpness[...] = row / math.sqrt(CHANNELS_PER_ATT)
    latents[lon] = latent[...]
    cots[lon] = cotangent[...]
    outer_t[...] = outer[...].astype(jnp.float32).T.astype(jnp.bfloat16)

    def perceptron(index, carry):
        rows = rows_of(index, CHUNK)
        pre_act = dot(tokens[rows, :], inner[...])
        sigmoid_val = jax.nn.sigmoid(pre_act)
        slope[rows, :] = sigmoid_val * (1.0 + pre_act * (1.0 - sigmoid_val))
        hidden_act = (pre_act * sigmoid_val).astype(jnp.bfloat16)
        hidden[rows, :] = hidden_act
        features[rows, :] = dot(hidden_act, outer[...]).astype(jnp.bfloat16)
        return carry

    lax.fori_loop(0, n_tokens // CHUNK, perceptron, 0)
    for copy in arriving[: n_lon - 1]:
        copy.wait()

    def prepare_queries(tile, carry):
        query = dot(latents[tile], projector[...]).astype(jnp.bfloat16).astype(jnp.float32)
        for group in range(groups):
            lanes = lanes_of(group)
            cell_t = spread_heads_t(latents[tile, :, lanes].astype(jnp.float32))
            spread_t = spread_heads_t(query[:, lanes])
            query_rows[tile, group] = spread_heads(query[:, lanes]).astype(jnp.bfloat16)
            query_cols[tile, group] = spread_t.astype(jnp.bfloat16)
            self_rows[tile, 0:1, lanes] = (
                jnp.sum(spread_t * cell_t, axis=0, keepdims=True) * sharpness[:, lanes])
        return carry

    lax.fori_loop(0, n_lon, prepare_queries, 0)
    for copy in arriving[n_lon - 1 :]:
        copy.wait()

    for tile in range(n_lon):
        cols = slice(tile * grid_cols, (tile + 1) * grid_cols)
        band[1 : 1 + grid_rows, cols, :] = (
            cots[tile].astype(jnp.float32).reshape(grid_rows, grid_cols, width))
        band[0, cols, :] = cots_above[tile].astype(jnp.float32)[16 - grid_cols :] * keep_above
        band[1 + grid_rows, cols, :] = cots_below[tile].astype(jnp.float32)[:grid_cols] * keep_below

    def mix_row(row, carry):
        for group in range(groups):
            lanes = lanes_of(group)
            mixed = band[1 + row, :, lanes]
            for index, (row_step, col_step) in enumerate(NEIGHBOURS):
                line = band[1 + row - row_step, :, lanes]
                if col_step:
                    line = pltpu.roll(line, col_step % (n_lon * grid_cols), 0)
                mixed = mixed + mixing[index : index + 1, lanes] * line
            mixed = mixed.astype(jnp.bfloat16).astype(jnp.float32)
            for tile in range(n_lon):
                grads[tile, rows_of(row, grid_cols), lanes] = (
                    mixed[tile * grid_cols : (tile + 1) * grid_cols])
        return carry

    lax.fori_loop(0, grid_rows, mix_row, 0)

    def prepare_grads(tile, carry):
        for group in range(groups):
            lanes = lanes_of(group)
            cell_t = spread_heads_t(latents[tile, :, lanes].astype(jnp.float32))
            spread_t = spread_heads_t(grads[tile, :, lanes])
            grad_rows[tile, group] = spread_heads(grads[tile, :, lanes]).astype(jnp.bfloat16)
            grad_cols[tile, group] = spread_t.astype(jnp.bfloat16)
            self_rows[tile, 1:2, lanes] = jnp.sum(spread_t * cell_t, axis=0, keepdims=True)
        return carry

    lax.fori_loop(0, n_lon, prepare_grads, 0)

    def block_sums(quad, carry):
        for block, group in [(4 * quad + i, j) for i in range(4) for j in range(groups)]:
            tile = targets[block]
            rows = rows_of(block, block_len)
            lanes = lanes_of(group)
            feature = features[rows, lanes]
            scores = dot(feature, query_cols[tile, group]) * sharpness[:, lanes]
            weight_grad = dot(feature, grad_cols[tile, group])
            if roomy:
                kept_scores[rows, lanes] = scores
                kept_grads[rows, lanes] = weight_grad
            top = jnp.max(scores, axis=0, keepdims=True)
            exp_terms = jnp.exp(scores - top)
            block_stats[block, 0:1, lanes] = top
            block_stats[block, 1:2, lanes] = jnp.sum(exp_terms, axis=0, keepdims=True)
            block_stats[block, 2:3, lanes] = jnp.sum(
                exp_terms * weight_grad, axis=0, keepdims=True)
        return carry

    lax.fori_loop(0, n_blocks // 4, block_sums, 0)

    for tile in range(n_lon):
        tops = [jnp.where(targets[block] == tile, block_stats[block, 0:1, :], LOWEST)
                for block in range(n_blocks)]
        top = functools.reduce(jnp.maximum, tops)
        exp_sum = jnp.zeros_like(top)
        grad_sum = jnp.zeros_like(top)
        for block in range(n_blocks):
            scale = jnp.exp(tops[block] - top)
            scale = jnp.where(targets[block] == tile, scale, 0.0)
            exp_sum = exp_sum + scale * block_stats[block, 1:2, :]
            grad_sum = grad_sum + scale * block_stats[block, 2:3, :]
        stats[lon, 4 * tile : 4 * tile + 1, :] = top
        stats[lon, 4 * tile + 1 : 4 * tile + 2, :] = exp_sum
        stats[lon, 4 * tile + 2 : 4 * tile + 3, :] = grad_sum
        stats[lon, 4 * tile + 3 : 4 * tile + 4, :] = jnp.zeros_like(top)

    arriving = [
        send(stats.at[lon], stats.at[lon], stat_send.at[step], stat_recv.at[step],
             (lat, sectors[step], mem))
        for step in range(1, n_lon)]
    update[...] = jnp.zeros_like(update)
    total[...] = jnp.zeros_like(total)
    for copy in arriving:
        copy.wait()

    for tile in range(n_lon):
        self_score = self_rows[tile, 0:1, :]
        top = self_score
        for sector in range(n_lon):
            top = jnp.maximum(top, stats[sector, 4 * tile : 4 * tile + 1, :])
        self_exp = jnp.exp(self_score - top)
        exp_sum = self_exp
        grad_sum = self_exp * self_rows[tile, 1:2, :]
        for sector in range(n_lon):
            scale = jnp.exp(stats[sector, 4 * tile : 4 * tile + 1, :] - top)
            exp_sum = exp_sum + scale * stats[sector, 4 * tile + 1 : 4 * tile + 2, :]
            grad_sum = grad_sum + scale * stats[sector, 4 * tile + 2 : 4 * tile + 3, :]
        inverse = 1.0 / exp_sum
        tile_stats[tile, 0:1, :] = top
        tile_stats[tile, 1:2, :] = inverse
        tile_stats[tile, 2:3, :] = grad_sum * inverse
        tile_stats[tile, 3:4, :] = self_exp * inverse

    def attend(quad, carry):
        for block, group in [(4 * quad + i, j) for i in range(4) for j in range(groups)]:
            tile = targets[block]
            rows = rows_of(block, block_len)
            lanes = lanes_of(group)
            feature = features[rows, lanes]
            if roomy:
                scores = kept_scores[rows, lanes]
                weight_grad = kept_grads[rows, lanes]
            else:
                scores = dot(feature, query_cols[tile, group]) * sharpness[:, lanes]
                weight_grad = dot(feature, grad_cols[tile, group])
            tile_rows = tile_stats[tile, :, lanes]
            probs = jnp.exp(scores - tile_rows[0:1]) * tile_rows[1:2]
            weights = probs.astype(jnp.bfloat16)
            logit_grad = (
                probs * (weight_grad - tile_rows[2:3]) * sharpness[:, lanes]
            ).astype(jnp.bfloat16)
            feature_grads[rows, lanes] = (
                dot(weights, grad_rows[tile, group]) + dot(logit_grad, query_rows[tile, group])
            ).astype(jnp.bfloat16)
            part = gather_heads(dot_rows(weights, feature), n_cells)
            for sector in range(n_lon):
                update[sector, :, lanes] += jnp.where(tile == sector, part, 0.0)
        return carry

    lax.fori_loop(0, n_blocks // 4, attend, 0)

    update_out[...] = update[...].astype(jnp.bfloat16)
    arriving = [
        send(update_out.at[sectors[step]], update_in.at[step], up_send.at[step], up_recv.at[step],
             (lat, sectors[step], mem))
        for step in range(1, n_lon)]

    def perceptron_grad(index, carry):
        rows = rows_of(index, CHUNK)
        feature_grad = feature_grads[rows, :]
        hidden_grad = (dot(feature_grad, outer_t[...]) * slope[rows, :]).astype(jnp.bfloat16)
        out_grad = dot_rows(hidden[rows, :], feature_grad)
        total[:GROUP, :GROUP] += dot_rows(tokens[rows, :], hidden_grad)
        total[:GROUP, GROUP:] += out_grad[:, :GROUP]
        total[GROUP:, :] += out_grad[:, GROUP:]
        return carry

    lax.fori_loop(0, n_tokens // CHUNK, perceptron_grad, 0)

    for copy in arriving:
        copy.wait()
    own_stats = tile_stats[lon]
    for group in range(groups):
        lanes = lanes_of(group)
        cells = latent[:, lanes].astype(jnp.float32)
        eye_shape = (GROUP, GROUP)
        eye = lax.broadcasted_iota(jnp.int32, eye_shape, 0) == lax.broadcasted_iota(
            jnp.int32, eye_shape, 1)
        self_weight = own_stats[3:4, lanes].astype(jnp.bfloat16).astype(jnp.float32)
        diagonal = jnp.where(eye, self_weight, 0.0).astype(jnp.bfloat16)
        own = dot(diagonal, spread_heads(cells).astype(jnp.bfloat16))
        change = update[lon, :, lanes] + gather_heads(own, n_cells)
        for step in range(1, n_lon):
            change = change + update_in[step, :, lanes].astype(jnp.float32)
        rounded = (cells + change).astype(jnp.bfloat16).astype(jnp.float32)
        state[:, :, lanes] = rounded.reshape(grid_rows, grid_cols, GROUP)
    for row in range(grid_rows):
        side[row : row + 1, :] = state[row, grid_cols - 1 : grid_cols, :]
        side[grid_rows + row : grid_rows + row + 1, :] = state[row, 0:1, :]
    rims_out[0] = state[0:2].reshape(16, width).astype(jnp.bfloat16)
    rims_out[1] = side[...].astype(jnp.bfloat16)
    rims_out[2] = state[grid_rows - 2 : grid_rows].reshape(16, width).astype(jnp.bfloat16)
    halos = []
    for index, (row_step, col_step) in enumerate(NEIGHBOURS):
        device = ((above, lat, below)[row_step + 1], lax.rem(lon + n_lon + col_step, n_lon), mem)
        halos.append(send(rims_out.at[row_step + 1], rims_in.at[index],
                          halo_send.at[index], halo_recv.at[index], device))

    whole = sum_over_devices(total, n_lat, n_lon, sum_refs)
    sums[...] = whole[...]

    for copy in halos:
        copy.wait()
    first, last = 8, 8 + grid_cols
    padded[1 : 1 + grid_rows, first:last, :] = state[...]
    for index, (row_step, col_step) in enumerate(NEIGHBOURS):
        rim = rims_in[index].astype(jnp.float32)
        if row_step == 0:
            place = first - 1 if col_step == 1 else last
            start = 0 if col_step == 1 else grid_rows
            for row in range(grid_rows):
                padded[1 + row, place : place + 1, :] = rim[start + row : start + row + 1]
        else:
            line = rim[16 - grid_cols :] * keep_above if row_step == 1 else rim[:grid_cols] * keep_below
            place = 0 if row_step == 1 else 1 + grid_rows
            if col_step == 0:
                padded[place, first:last, :] = line
            elif col_step == 1:
                padded[place, first - 1 : first, :] = line[grid_cols - 1 :]
            else:
                padded[place, last : last + 1, :] = line[:1]
    for group in range(groups):
        lanes = lanes_of(group)
        mixed = padded[1 : 1 + grid_rows, first:last, lanes]
        for index, (row_step, col_step) in enumerate(NEIGHBOURS):
            mixed = mixed + mixing[index : index + 1, lanes] * padded[
                1 + row_step : 1 + row_step + grid_rows, first + col_step : last + col_step, lanes]
        analysis[:, lanes] = mixed.reshape(n_cells, GROUP).astype(jnp.bfloat16)


def finish_kernel(analysis, sums, analysis_out, in_sum, out_sum):
    analysis_out[...] = analysis[...]
    in_sum[...] = sums[0, :, :GROUP].astype(jnp.float32)
    out_sum[:, :GROUP] = sums[0, :, GROUP:].astype(jnp.float32)
    out_sum[:, GROUP:] = sums[1].astype(jnp.float32)


def per_device(
    measured_inputs,
    target_sector,
    hidden_member_fields,
    analysis_adjoint,
    inner_perceptron_coeffs,
    outer_perceptron_coeffs,
    probe_projector,
    logit_sharpness,
    adjacent_channel_coeffs,
):
    n_lat, n_lon = lax.axis_size("lat"), lax.axis_size("lon")
    n_blocks, block_len, obs_width = measured_inputs.shape
    grid_rows, grid_cols, width = hidden_member_fields.shape[1:]
    hidden_width = inner_perceptron_coeffs.shape[1]
    n_cells = grid_rows * grid_cols
    n_tokens = n_blocks * block_len
    groups = width // GROUP
    roomy = n_lon <= 4
    bf16, f32 = jnp.bfloat16, jnp.float32
    vmem, dma = pltpu.VMEM, pltpu.SemaphoreType.DMA
    in_vmem = pl.BlockSpec(memory_space=pltpu.VMEM)
    spread = vmem((n_lon, groups, GROUP, GROUP), bf16)
    scratch = [
        vmem((n_lon, n_cells, width), bf16),
        vmem((n_lon, n_cells, width), bf16),
        vmem((n_lon, 16, width), bf16),
        vmem((n_lon, 16, width), bf16),
        vmem((grid_rows + 2, n_lon * grid_cols, width), f32),
        vmem((width, hidden_width), bf16),
        spread, spread, spread, spread,
        vmem((n_lon, 8, width), f32),
        vmem((n_tokens, width), bf16),
        vmem((n_tokens if roomy else 16, width), bf16),
        vmem((n_tokens if roomy else 8, width), f32),
        vmem((n_tokens if roomy else 8, width), f32),
        vmem((1, width), f32),
        vmem((n_tokens, hidden_width), bf16),
        vmem((n_tokens, hidden_width), f32),
        vmem((n_blocks, 8, width), f32),
        vmem((n_lon, 4 * n_lon, width), f32),
        vmem((n_lon, 8, width), f32),
        vmem((n_lon, n_cells, width), f32),
        vmem((n_lon, n_cells, width), bf16),
        vmem((n_lon, n_cells, width), bf16),
        vmem((grid_rows, grid_cols, width), f32),
        vmem((16, width), f32),
        vmem((3, 16, width), bf16),
        vmem((8, 16, width), bf16),
        vmem((grid_rows + 2, 24, width), f32),
        vmem((2 * GROUP, 2 * GROUP), f32),
        dma((n_lon,)), dma((n_lon,)), dma((n_lon,)), dma((n_lon,)),
        dma((2, n_lon)), dma((2, n_lon)),
        dma((n_lon,)), dma((n_lon,)), dma((n_lon,)), dma((n_lon,)),
        dma((8,)), dma((8,)),
    ] + sum_scratch(n_lat, n_lon, 2 * GROUP, 2 * GROUP)
    in_smem = pl.BlockSpec(memory_space=pltpu.SMEM)
    analysis, sums = pl.pallas_call(
        functools.partial(step_kernel, n_lat, n_lon, n_blocks, grid_rows, grid_cols, roomy),
        out_shape=[
            jax.ShapeDtypeStruct((n_cells, width), bf16),
            jax.ShapeDtypeStruct((2, GROUP, 2 * GROUP), bf16),
        ],
        in_specs=[in_smem] * 2 + [in_vmem] * 7,
        out_specs=[in_vmem] * 2,
        scratch_shapes=scratch,
        compiler_params=pltpu.CompilerParams(
            collective_id=0, has_side_effects=True, vmem_limit_bytes=60 << 20
        ),
        name="assimilation_step",
    )(
        target_sector,
        logit_sharpness,
        measured_inputs.reshape(n_tokens, obs_width),
        hidden_member_fields.reshape(n_cells, width),
        analysis_adjoint.reshape(n_cells, width),
        inner_perceptron_coeffs,
        outer_perceptron_coeffs,
        probe_projector,
        adjacent_channel_coeffs,
    )
    analysis, in_grad, out_grad = pl.pallas_call(
        finish_kernel,
        out_shape=[
            jax.ShapeDtypeStruct((n_cells, width), bf16),
            jax.ShapeDtypeStruct(inner_perceptron_coeffs.shape, f32),
            jax.ShapeDtypeStruct(outer_perceptron_coeffs.shape, f32),
        ],
        in_specs=[in_vmem] * 2,
        out_specs=[in_vmem] * 3,
        compiler_params=pltpu.CompilerParams(vmem_limit_bytes=16 << 20),
        name="to_float32",
    )(analysis, sums)
    return (analysis.reshape(hidden_member_fields.shape), in_grad, out_grad)


def solution(mesh):
    in_specs = (
        P(("lat", "lon", "mem"), None, None),
        P(("lat", "lon", "mem")),
        P("mem", "lat", "lon", None),
        P("mem", "lat", "lon", None),
        P(),
        P(),
        P(),
        P(),
        P(),
    )
    out_specs = (P("mem", "lat", "lon", None), P(), P())
    return jax.shard_map(
        per_device, mesh=mesh, in_specs=in_specs, out_specs=out_specs, check_vma=False
    )
```
